128 devices in a mesh: seq: 16 (over z, x), tp: 8 (over y, core).
Axes of the slice: x: 4, y: 4, z: 4, core: 2. Of those that a mesh axis runs over, the one named last changes fastest.
Arguments:
- inner_x: bfloat16 [4, 2048, 8192], P(None, 'seq', 'tp'), may hold values from -6 to 6
- inner_z: bfloat16 [4, 2048, 8192], P(None, 'seq', 'tp'), may hold values from -6 to 6
- conv_tail: bfloat16 [4, 3, 8192], P(None, None, 'tp'), may hold values from -6 to 6
- conv_weight: float32 [4, 8192], P(None, 'tp'), may hold values from -3 to 3
- conv_bias: float32 [8192], P('tp'), may hold values from -3 to 3
- xproj_dt: bfloat16 [8192, 512], P('tp'), may hold values from -0.0625 to 0.0625
- xproj_bc: bfloat16 [8192, 32], P('tp'), may hold values from -0.0625 to 0.0625
- dt_weight: bfloat16 [512, 8192], P(None, 'tp'), may hold values from -0.25 to 0.25
- dt_bias: float32 [8192], P('tp'), may hold values from -5 to -4
- decay_log: float32 [16, 8192], P(None, 'tp'), may hold values from -8 to 1.1
- skip_gain: float32 [8192], P('tp'), may hold values from 0.5 to 1.5
- out_weight: bfloat16 [8192, 8192], P('tp'), may hold values from -0.0625 to 0.0625
- residual: bfloat16 [4, 2048, 8192], P(None, 'seq', 'tp'), may hold values from -6 to 6
- init_state: float32 [4, 16, 8192], P(None, None, 'tp'), may hold values from -6 to 6
Outputs:
- hidden_out: bfloat16 [4, 2048, 8192], P(None, 'seq', 'tp')
- block_states: float32 [16, 4, 16, 8192], P('seq', None, None, 'tp')
The draws below stay inside these ranges and needn't reach their ends.
All inputs are finite; a program needn't handle non-finite values.
Results may differ from the reference program's by a relative error of at most 0.024.
Values may be sent and summed in bfloat16 or wider, within the bound.
A program may use at most 128 MiB of HBM per device.

```python
import jax
import jax.numpy as jnp
from jax import lax

D = 8192
DI = 8192
R = 512
NS = 16
KCONV = 4
SEQS = 4
TOK_BLK = 128
LEN = 2048
N_SEQ = 16
N_TP = 8


def draw_decay_log(key, part):
    folded = jax.random.fold_in(key, 7)
    choose_key, level_key = jax.random.split(folded)
    share_slow = 0.5
    slow_mask = jax.random.bernoulli(choose_key, share_slow, (1, DI))
    levels = jax.random.uniform(level_key, (NS, DI), jnp.float32)
    slow_log = jnp.log(5.0 / LEN) + levels * jnp.log(10.0)
    fast_log = levels * jnp.log(3.0)
    return jnp.where(slow_mask, slow_log, fast_log).astype(jnp.float32)


def block_scale(stream_key, shape, pieces, smallest, largest):
    gain = 1.0
    for axis_at, blocks in pieces:
        steps = jax.random.uniform(jax.random.fold_in(jax.random.fold_in(stream_key, 6), axis_at), (blocks,), jnp.float32, smallest / len(pieces), largest / len(pieces))
        gain = gain * jnp.repeat(jnp.exp(steps), shape[axis_at] // blocks).reshape((-1,) + (1,) * (len(shape) - 1 - axis_at))
    return gain


def centred(key, extent, width, most, shards=(), held_as=jnp.bfloat16):
    gain = block_scale(key, extent, shards, -0.22, 0.18) if shards else 1.0
    entries = jax.random.normal(key, extent, jnp.float32) * width * gain
    return jnp.minimum(jnp.maximum(entries, -most), most).astype(held_as)


def setup_inputs(seed: int = 0) -> dict:
    arg_keys = jax.random.split(jax.random.key(seed), 15)
    return {
        "inner_x": centred(arg_keys[0], (SEQS, LEN, DI), 1.0, 6.0, ((1, 16), (2, 8))),
        "inner_z": centred(arg_keys[1], (SEQS, LEN, DI), 1.0, 6.0, ((1, 16), (2, 8))),
        "conv_tail": centred(arg_keys[2], (SEQS, KCONV - 1, DI), 1.0, 6.0, ((2, 8),)),
        "conv_weight": centred(arg_keys[3], (KCONV, DI), KCONV ** -0.5, 3.0, ((1, 8),), jnp.float32),
        "conv_bias": centred(arg_keys[4], (DI,), 0.5, 3.0, ((0, 8),), jnp.float32),
        "xproj_dt": centred(arg_keys[5], (DI, R), DI ** -0.5, 0.0625, ((0, 8),)),
        "xproj_bc": centred(arg_keys[6], (DI, 2 * NS), DI ** -0.5, 0.0625, ((0, 8),)),
        "dt_weight": centred(arg_keys[7], (R, DI), R ** -0.5, 0.25, ((1, 8),)),
        "dt_bias": jnp.clip(-5.0 + 1.0 * jax.random.uniform(arg_keys[8], (DI,), jnp.float32) ** block_scale(arg_keys[8], (DI,), ((0, 8),), -0.2, 0.2), -5.0, -4.0),
        "decay_log": draw_decay_log(jax.random.fold_in(arg_keys[14], 71), 0),
        "skip_gain": jnp.clip(0.5 + 1.0 * jax.random.uniform(arg_keys[10], (DI,), jnp.float32) ** block_scale(arg_keys[10], (DI,), ((0, 8),), -0.2, 0.2), 0.5, 1.5),
        "out_weight": centred(arg_keys[11], (DI, D), DI ** -0.5, 0.0625, ((0, 8),)),
        "residual": centred(arg_keys[12], (SEQS, LEN, D), 1.0, 6.0, ((1, 16), (2, 8))),
        "init_state": centred(arg_keys[13], (SEQS, NS, DI), 1.0, 6.0, ((2, 8),), jnp.float32),
    }


def matmul(left_op, right_op):
    return jnp.dot(left_op.astype(jnp.float32), right_op.astype(jnp.float32), preferred_element_type=jnp.float32)

def run_chain(initial, decay_rates, steps_dt, inputs_x, gates_b, reads_c):

    def advance(carried, packed):
        step_dt, value_x, gate_b, read_c = packed
        factor = jnp.exp(decay_rates[None, :, :] * step_dt[:, None, :])
        carried = factor * carried + (step_dt * value_x)[:, None, :] * gate_b[:, :, None]
        emitted = lax.optimization_barrier(jnp.sum(read_c[:, :, None] * carried, axis=1))
        return (carried, emitted)
    return lax.scan(advance, initial, (steps_dt, inputs_x, gates_b, reads_c), unroll=8)

def reference(inner_x, inner_z, conv_tail, conv_weight, conv_bias, xproj_dt, xproj_bc, dt_weight, dt_bias, decay_log, skip_gain, out_weight, residual, init_state):
    length = inner_x.shape[1]
    joined = jnp.concatenate([conv_tail, inner_x], axis=1).astype(jnp.float32)
    conv_mixed = conv_bias + conv_weight[0] * joined[:, 0:length, :]
    for offset in range(1, KCONV):
        conv_mixed = conv_mixed + conv_weight[offset] * joined[:, offset:offset + length, :]
    conv_act = jax.nn.silu(conv_mixed).astype(jnp.bfloat16)
    low_rank = matmul(conv_act, xproj_dt)
    bc_proj = matmul(conv_act, xproj_bc)
    normed = (low_rank * lax.rsqrt(lax.optimization_barrier(jnp.mean(low_rank * low_rank, axis=-1, keepdims=True)) + 1e-06)).astype(jnp.bfloat16)
    steps_dt = jax.nn.softplus(matmul(normed, dt_weight) + dt_bias)
    gates_b = bc_proj[..., :NS]
    reads_c = bc_proj[..., NS:]
    decay_rates = -jnp.exp(decay_log)
    values = conv_act.astype(jnp.float32)

    def to_blocks(array_in):
        return jnp.transpose(array_in, (1, 0, 2)).reshape(N_SEQ, TOK_BLK, array_in.shape[0], array_in.shape[2])

    def per_block(carried, packed):
        carried, emitted = run_chain(carried, decay_rates, packed[0], packed[1], packed[2], packed[3])
        return (carried, (carried, emitted))
    unused, (states, emitted) = lax.scan(per_block, init_state, (to_blocks(steps_dt), to_blocks(values), to_blocks(gates_b), to_blocks(reads_c)))
    scanned = jnp.transpose(emitted.reshape(length, SEQS, -1), (1, 0, 2)) + skip_gain * values
    gated_out = (scanned * jax.nn.silu(inner_z.astype(jnp.float32))).astype(jnp.bfloat16)
    group_width = DI // N_TP
    total_sum = jnp.zeros(residual.shape, jnp.float32)
    for group_index in range(N_TP):
        lower = group_index * group_width
        partial_sum = matmul(gated_out[..., lower:lower + group_width], out_weight[lower:lower + group_width]).astype(jnp.bfloat16)
        partial_sum = lax.optimization_barrier(partial_sum)
        total_sum = total_sum + partial_sum.astype(jnp.float32)
    hidden_out = (residual.astype(jnp.float32) + total_sum).astype(jnp.bfloat16)
    return (hidden_out, states)
```

```python
import jax
import jax.numpy as jnp
from jax import lax
from jax.experimental import pallas as pl
from jax.experimental.pallas import tpu as pltpu
from jax.sharding import PartitionSpec as P

MESH = pl.DeviceIdType.MESH
F32 = jnp.float32
BF16 = jnp.bfloat16
LOG2E = 1.4426950408889634

N_SEQ = 16
N_TP = 8
N_Y = 4
SEQS = 4
TOK = 128
CH = 1024
NG = CH // 128
RANK = 512
LOWW = RANK + 128
NS = 16
GROUPS = 2
GS = SEQS // GROUPS
OWN = TOK // N_TP
ROWS = SEQS * TOK
GROWS = GS * TOK
HALF = TOK // 2


def mix_kernel(
    x_ref,
    tail_ref,
    cw_ref,
    cb_ref,
    xdt_ref,
    xbc_ref,
    dtb_ref,
    decay_ref,
    skip_ref,
    init_ref,
    z_hbm,
    dtw_hbm,
    w_hbm,
    res_hbm,
    out_ref,
    st_ref,
    z_ref,
    dtw_ref,
    w_ref,
    res_ref,
    rim_out,
    rim_in,
    joined,
    act,
    xg,
    dtg,
    splat,
    rate_t,
    init_t,
    flip,
    lowp,
    lowr,
    lown,
    exs,
    exr,
    rets,
    ent,
    snd,
    rcv,
    opp,
    fin,
    load_sem,
    rim_ssem,
    rim_rsem,
    low_ssem,
    low_rsem,
    nrm_ssem,
    nrm_rsem,
    ex_ssem,
    ex_rsem,
    ret_ssem,
    ret_rsem,
    sib_ssem,
    sib_rsem,
    opp_ssem,
    opp_rsem,
    fin_ssem,
    fin_rsem,
):
    q = lax.axis_index("seq")
    t = lax.axis_index("tp")
    y = t // 2
    core = lax.rem(t, 2)

    def on_tp(p):
        return (q, p)

    def on_seq(p):
        return (p, t)

    sib = on_tp(y * 2 + 1 - core)
    up = on_tp(lax.rem(y + 1, N_Y) * 2 + core)
    down = on_tp(lax.rem(y + N_Y - 1, N_Y) * 2 + core)

    def remote(src, dst, ssem, rsem, dev):
        return pltpu.make_async_remote_copy(
            src_ref=src, dst_ref=dst, send_sem=ssem, recv_sem=rsem, device_id=dev, device_id_type=MESH
        )

    loads = [
        pltpu.make_async_copy(dtw_hbm, dtw_ref, load_sem.at[0]),
        pltpu.make_async_copy(z_hbm, z_ref, load_sem.at[1]),
        pltpu.make_async_copy(w_hbm, w_ref, load_sem.at[2]),
        pltpu.make_async_copy(res_hbm, res_ref, load_sem.at[3]),
    ]
    for c in loads:
        c.start()

    barrier = pltpu.get_barrier_semaphore()
    for k in range(1, N_TP):
        pl.semaphore_signal(barrier, inc=1, device_id=on_tp(lax.rem(t + k, N_TP)), device_id_type=MESH)
    for k in range(1, N_SEQ):
        pl.semaphore_signal(barrier, inc=1, device_id=on_seq(lax.rem(q + k, N_SEQ)), device_id_type=MESH)

    row8 = lax.broadcasted_iota(jnp.int32, (8, CH), 0)
    last = [x_ref[s, TOK - 16 : TOK, :].astype(F32)[8:16, :] for s in range(SEQS)]
    packed = [jnp.where(row8 < 4, pltpu.roll(last[s], 4, 0), last[s + 1]) for s in (0, 2)]
    rim_out[...] = jnp.concatenate(packed, axis=0).astype(BF16)

    pl.semaphore_wait(barrier, N_TP - 1 + N_SEQ - 1)
    rim = remote(rim_out, rim_in, rim_ssem, rim_rsem, on_seq(lax.rem(q + 1, N_SEQ)))
    rim.start()

    for g in range(GROUPS):
        lowp[g * GROWS : (g + 1) * GROWS, RANK:] = jnp.zeros((GROWS, LOWW - RANK), BF16)

    for nb in range(NS // 8):
        for c in range(NG):
            flip[c * 8 : (c + 1) * 8, :] = -jnp.exp(decay_ref[nb * 8 : nb * 8 + 8, c * 128 : (c + 1) * 128]) * LOG2E
        for i in range(8):
            rate_t[nb * 8 + i] = flip[pl.ds(i, 8, stride=8), :]

    @pl.loop(0, SEQS)
    def _(s):
        for nb in range(NS // 8):
            for c in range(NG):
                flip[c * 8 : (c + 1) * 8, :] = init_ref[s, nb * 8 : nb * 8 + 8, c * 128 : (c + 1) * 128]
            for i in range(8):
                init_t[s, nb * 8 + i] = flip[pl.ds(i, 8, stride=8), :]

    def widen(s):
        @pl.loop(0, TOK // 16)
        def _(b):
            r = pl.multiple_of(b * 16, 16)
            joined[s, pl.ds(r + 8, 16), :] = x_ref[s, pl.ds(r, 16), :].astype(F32)

    def conv_block(s, b):
        r = pl.multiple_of(b * 16, 16)
        window = joined[s, pl.ds(r, 24), :]
        mixed = cb_ref[...] + cw_ref[0:1, :] * window[5:21, :]
        for k in range(1, 4):
            mixed = mixed + cw_ref[k : k + 1, :] * window[5 + k : 21 + k, :]
        rounded = (mixed / (1.0 + jnp.exp(-mixed))).astype(BF16)
        act[pl.ds(s * TOK + r, 16), :] = rounded
        wide = rounded.astype(F32)
        for h in range(2):
            base = pl.multiple_of((s * (TOK // 8) + b * 2 + h) * 64, 64)
            for c in range(NG):
                xg[pl.ds(base + c * 8, 8), :] = wide[h * 8 : h * 8 + 8, c * 128 : (c + 1) * 128]

    def low_copy(g, k):
        p = lax.rem(t + k, N_TP)
        return [
            remote(
                lowp.at[pl.ds((g * GS + s) * TOK + pl.multiple_of(p * OWN, OWN), OWN), :],
                lowr.at[g, k - 1, s],
                low_ssem.at[g, k - 1, s],
                low_rsem.at[g, k - 1, s],
                on_tp(p),
            )
            for s in range(GS)
        ]

    def nrm_copy(g, k):
        p = lax.rem(t + k, N_TP)
        out = []
        for s in range(GS):
            rows = pl.ds((g * GS + s) * TOK + pl.multiple_of(t * OWN, OWN), OWN)
            out.append(
                remote(
                    lown.at[rows, :], lown.at[rows, :], nrm_ssem.at[g, k - 1, s], nrm_rsem.at[g, k - 1, s], on_tp(p)
                )
            )
        return out

    def ex_copy(g, k):
        p = lax.rem(q + k, N_SEQ)
        return remote(exs.at[g, p], exr.at[g, q], ex_ssem.at[g, k - 1], ex_rsem.at[g, k - 1], on_seq(p))

    def ret_copy(g, k):
        p = lax.rem(q + k, N_SEQ)
        return remote(rets.at[g, p], ent.at[g, q], ret_ssem.at[g, k - 1], ret_rsem.at[g, k - 1], on_seq(p))

    for g in range(GROUPS):
        for s in range(g * GS, (g + 1) * GS):
            widen(s)

            @pl.loop(1, TOK // 16)
            def _(b):
                conv_block(s, b)

        if g == 0:
            rim.wait()
            for s in range(SEQS):
                part = rim_in[...].astype(F32)[(s // 2) * 8 : (s // 2) * 8 + 8, :]
                joined[s, 0:8, :] = pltpu.roll(part, 4, 0) if s % 2 == 0 else part

            @pl.when(q == 0)
            def _():
                for s in range(SEQS):
                    joined[s, 5:8, :] = tail_ref[s].astype(F32)

        for s in range(g * GS, (g + 1) * GS):
            conv_block(s, 0)
        rows = slice(g * GROWS, (g + 1) * GROWS)
        lowp[rows, 0:RANK] = jnp.dot(act[rows, :], xdt_ref[...], preferred_element_type=F32).astype(BF16)
        lowp[rows, RANK : RANK + 2 * NS] = jnp.dot(
            act[rows, :], xbc_ref[...], preferred_element_type=F32
        ).astype(BF16)
        for k in range(1, N_TP):
            for c in low_copy(g, k):
                c.start()

    for g in range(GROUPS):
        for k in range(1, N_TP):
            for c in low_copy(g, k):
                c.wait_recv()
        for s in range(GS):
            rows = pl.ds((g * GS + s) * TOK + pl.multiple_of(t * OWN, OWN), OWN)
            total = lowp[rows, :].astype(F32)
            for k in range(N_TP - 1):
                total = total + lowr[g, k, s].astype(F32)
            low = total[:, :RANK]
            scale = lax.rsqrt(jnp.mean(low * low, axis=-1, keepdims=True) + 1e-6)
            lown[rows, 0:RANK] = (low * scale).astype(BF16)
            bc = total[:, RANK:]
            high = bc.astype(BF16).astype(F32)
            lown[rows, RANK:] = (high + pltpu.roll(bc - high, 2 * NS, 1)).astype(BF16)
        for k in range(1, N_TP):
            for c in nrm_copy(g, k):
                c.start()

    loads[0].wait()

    def steps(g):
        base = g * GROWS

        @pl.loop(0, CH // 256)
        def _(nc):
            cols = pl.ds(pl.multiple_of(nc * 256, 256), 256)
            pre = (
                jnp.dot(lown[base : base + GROWS, 0:RANK], dtw_ref[:, cols], preferred_element_type=F32)
                + dtb_ref[:, cols]
            )
            dt = jnp.maximum(pre, 0.0) + jnp.log1p(jnp.exp(-jnp.abs(pre)))
            for b in range(GROWS // 8):
                for h in range(2):
                    at = pl.multiple_of((base // 8 + b) * 64 + (nc * 2 + h) * 8, 8)
                    dtg[pl.ds(at, 8), :] = dt[b * 8 : b * 8 + 8, h * 128 : (h + 1) * 128]

        @pl.loop(0, NS)
        def _(p):
            r = lax.broadcasted_iota(jnp.int32, (128, 256), 0)
            n = lax.broadcasted_iota(jnp.int32, (128, 256), 1) // 128 + 2 * p
            pick = jnp.where((r == n) | (r == n + 2 * NS), 1.0, 0.0).astype(BF16)
            wide = jnp.dot(lown[base : base + GROWS, RANK:], pick, preferred_element_type=F32)
            for h in range(2):
                at = pl.multiple_of((2 * p + h) * ROWS + base, GROWS)
                splat[pl.ds(at, GROWS), :] = wide[:, h * 128 : h * 128 + 128]

    def first_pass(g, sl):
        s = g * GS + sl
        rates = [rate_t[n] for n in range(NS)]

        def block(b, carry):
            h, elapsed = list(carry[0]), carry[1]
            base = pl.multiple_of((s * (TOK // 8) + b) * 64, 64)
            for i in range(8):
                dt = dtg[pl.ds(base + i, 8, stride=8), :]
                u = dt * xg[pl.ds(base + i, 8, stride=8), :]
                elapsed = elapsed + dt
                tok = s * TOK + b * 8 + i
                for n in range(NS):
                    h[n] = jnp.exp2(rates[n] * dt) * h[n] + splat[pl.ds(n * ROWS + tok, 1), :] * u
            return (tuple(h), elapsed)

        zero = jnp.zeros((8, 128), F32)
        h, elapsed = lax.fori_loop(0, TOK // 8, block, ((zero,) * NS, zero))
        for n in range(NS):
            pair = jnp.concatenate([h[n], jnp.exp2(rates[n] * elapsed)], axis=0).astype(BF16)
            exs[g, n, sl * 16 : (sl + 1) * 16, :] = pair

    for g in range(GROUPS):
        for k in range(1, N_TP):
            for c in nrm_copy(g, k):
                c.wait_recv()
        steps(g)
        for sl in range(GS):
            first_pass(g, sl)
        exr[g, q] = exs[g, q]
        for k in range(1, N_SEQ):
            ex_copy(g, k).start()

    for g in range(GROUPS):
        for k in range(1, N_SEQ):
            ex_copy(g, k).wait_recv()
        for sl in range(GS):
            h = init_t[g * GS + sl, q]
            for i in range(N_SEQ):
                rets[g, i, sl * 8 : sl * 8 + 8, :] = h
                pair = exr[g, i, sl * 16 : (sl + 1) * 16, :].astype(F32)
                h = pair[8:16] * h + pair[0:8]
        ent[g, q] = rets[g, q]
        for k in range(1, N_SEQ):
            ret_copy(g, k).start()

    def second_pass(s):
        g, sl = s // GS, s % GS
        rates = [rate_t[n] for n in range(NS)]
        skip = skip_ref[...]

        def block(b, h):
            h = list(h)
            base = pl.multiple_of((s * (TOK // 8) + b) * 64, 64)
            for i in range(8):
                dt = dtg[pl.ds(base + i, 8, stride=8), :]
                v = xg[pl.ds(base + i, 8, stride=8), :]
                u = dt * v
                tok = s * TOK + b * 8 + i
                total = skip * v
                for n in range(NS):
                    h[n] = jnp.exp2(rates[n] * dt) * h[n] + splat[pl.ds(n * ROWS + tok, 1), :] * u
                    total = total + splat[pl.ds((NS + n) * ROWS + tok, 1), :] * h[n]
                xg[pl.ds(base + i, 8, stride=8), :] = total
            return tuple(h)

        h = lax.fori_loop(0, TOK // 8, block, tuple(ent[g, n, sl * 8 : sl * 8 + 8, :] for n in range(NS)))
        for nb in range(NS // 8):
            for i in range(8):
                flip[pl.ds(i, 8, stride=8), :] = h[nb * 8 + i]
            for c in range(NG):
                st_ref[0, s, nb * 8 : nb * 8 + 8, c * 128 : (c + 1) * 128] = flip[c * 8 : (c + 1) * 8, :]

    def gate(s):
        @pl.loop(0, TOK // 16)
        def _(b):
            r = pl.multiple_of(b * 16, 16)
            z = z_ref[s, pl.ds(r, 16), :].astype(F32)
            sz = z / (1.0 + jnp.exp(-z))
            base = pl.multiple_of((s * (TOK // 8) + b * 2) * 64, 64)
            for c in range(NG):
                scanned = jnp.concatenate(
                    [xg[pl.ds(base + c * 8, 8), :], xg[pl.ds(base + 64 + c * 8, 8), :]], axis=0
                )
                act[pl.ds(s * TOK + r, 16), c * 128 : (c + 1) * 128] = (
                    scanned * sz[:, c * 128 : (c + 1) * 128]
                ).astype(BF16)

    def columns(j, who, n):
        dest = lax.rem(y + j, N_Y) * 2 + who
        return pl.ds(pl.multiple_of(dest * CH + n * 256, 256), 256)

    def product(s, j, who, n):
        return jnp.dot(
            act[s * TOK : (s + 1) * TOK, :], w_ref[:, columns(j, who, n)], preferred_element_type=F32
        )

    def sib_copy(s, j):
        return remote(snd.at[s, j], rcv.at[s, j], sib_ssem.at[s, j], sib_rsem.at[s, j], sib)

    lo, hi = pl.ds(0, HALF), pl.ds(HALF, HALF)

    def opp_copies(s):
        return (
            remote(rcv.at[s, 2, lo], opp.at[s, 0], opp_ssem.at[s, 0], opp_rsem.at[s, 0], up),
            remote(rcv.at[s, 2, hi], opp.at[s, 1], opp_ssem.at[s, 1], opp_rsem.at[s, 1], down),
        )

    def own_up(s):
        return remote(rcv.at[s, 1, hi], fin.at[s, 0, hi], fin_ssem.at[s, 0], fin_rsem.at[s, 0], up)

    def own_down(s):
        return remote(rcv.at[s, 3, lo], fin.at[s, 1, lo], fin_ssem.at[s, 1], fin_rsem.at[s, 1], down)

    def fwd_copies(s):
        return (
            remote(rcv.at[s, 1, lo], fin.at[s, 0, lo], fin_ssem.at[s, 2], fin_rsem.at[s, 2], up),
            remote(rcv.at[s, 3, hi], fin.at[s, 1, hi], fin_ssem.at[s, 3], fin_rsem.at[s, 3], down),
        )

    def for_sibling(s):
        for j in (2, 1, 3, 0):

            @pl.loop(0, CH // 256)
            def _(n):
                cols = pl.ds(pl.multiple_of(n * 256, 256), 256)
                snd[s, j, :, cols] = product(s, j, 1 - core, n).astype(BF16)

            sib_copy(s, j).start()

    def for_chip(s):
        for j in (2, 1, 3, 0):
            sib_copy(s, j).wait_recv()

            @pl.loop(0, CH // 256)
            def _(n):
                cols = pl.ds(pl.multiple_of(n * 256, 256), 256)
                rcv[s, j, :, cols] = (product(s, j, core, n) + rcv[s, j, :, cols].astype(F32)).astype(BF16)

            if j == 2:
                for c in opp_copies(s):
                    c.start()
            if j == 1:
                own_up(s).start()
            if j == 3:
                own_down(s).start()

    def forward(s):
        for d, (arriving, c) in enumerate(zip(opp_copies(s), fwd_copies(s))):
            arriving.wait_recv()
            j, r0 = (1, 0) if d == 0 else (3, HALF)

            @pl.loop(0, HALF // 16)
            def _(b):
                r = pl.multiple_of(b * 16, 16)
                mine = rcv[s, j, pl.ds(r0 + r, 16), :].astype(F32)
                rcv[s, j, pl.ds(r0 + r, 16), :] = (mine + opp[s, d, pl.ds(r, 16), :].astype(F32)).astype(BF16)

            c.start()

    def finish(s):
        for c in (own_up(s), own_down(s)) + fwd_copies(s):
            c.wait_recv()

        @pl.loop(0, TOK // 16)
        def _(b):
            r = pl.ds(pl.multiple_of(b * 16, 16), 16)
            total = res_ref[s, r, :].astype(F32) + rcv[s, 0, r, :].astype(F32)
            total = total + fin[s, 0, r, :].astype(F32) + fin[s, 1, r, :].astype(F32)
            out_ref[s, r, :] = total.astype(BF16)

    for s in range(SEQS):
        if s % GS == 0:
            for k in range(1, N_SEQ):
                ret_copy(s // GS, k).wait_recv()
        second_pass(s)
        if s == 0:
            loads[1].wait()
            loads[2].wait()
        gate(s)
        for_sibling(s)
        if s > 0:
            forward(s - 1)
        for_chip(s)
        if s == 1:
            loads[3].wait()
        if s > 1:
            finish(s - 2)
    forward(SEQS - 1)
    finish(SEQS - 2)
    finish(SEQS - 1)

    for g in range(GROUPS):
        for k in range(1, N_TP):
            for c in low_copy(g, k) + nrm_copy(g, k):
                c.wait_send()
        for k in range(1, N_SEQ):
            ex_copy(g, k).wait_send()
            ret_copy(g, k).wait_send()
    for s in range(SEQS):
        for j in range(N_Y):
            sib_copy(s, j).wait_send()
        for c in opp_copies(s) + (own_up(s), own_down(s)) + fwd_copies(s):
            c.wait_send()


def body(
    inner_x,
    inner_z,
    conv_tail,
    conv_weight,
    conv_bias,
    xproj_dt,
    xproj_bc,
    dt_weight,
    dt_bias,
    decay_log,
    skip_gain,
    out_weight,
    residual,
    init_state,
):
    vmem = pl.BlockSpec(memory_space=pltpu.VMEM)
    anym = pl.BlockSpec(memory_space=pl.ANY)
    dma = pltpu.SemaphoreType.DMA
    scratch = [
        pltpu.VMEM((SEQS, TOK, CH), BF16),
        pltpu.VMEM((RANK, CH), BF16),
        pltpu.VMEM((CH, N_TP * CH), BF16),
        pltpu.VMEM((SEQS, TOK, CH), BF16),
        pltpu.VMEM((16, CH), BF16),
        pltpu.VMEM((16, CH), BF16),
        pltpu.VMEM((SEQS, TOK + 8, CH), F32),
        pltpu.VMEM((ROWS, CH), BF16),
        pltpu.VMEM((ROWS * 8, 128), F32),
        pltpu.VMEM((ROWS * 8, 128), F32),
        pltpu.VMEM((2 * NS * ROWS, 128), F32),
        pltpu.VMEM((NS, 8, 128), F32),
        pltpu.VMEM((SEQS, NS, 8, 128), F32),
        pltpu.VMEM((64, 128), F32),
        pltpu.VMEM((ROWS, LOWW), BF16),
        pltpu.VMEM((GROUPS, N_TP - 1, GS, OWN, LOWW), BF16),
        pltpu.VMEM((ROWS, LOWW), BF16),
        pltpu.VMEM((GROUPS, NS, GS * 16, 128), BF16),
        pltpu.VMEM((GROUPS, N_SEQ, GS * 16, 128), BF16),
        pltpu.VMEM((GROUPS, N_SEQ, GS * 8, 128), F32),
        pltpu.VMEM((GROUPS, NS, GS * 8, 128), F32),
        pltpu.VMEM((SEQS, N_Y, TOK, CH), BF16),
        pltpu.VMEM((SEQS, N_Y, TOK, CH), BF16),
        pltpu.VMEM((SEQS, 2, HALF, CH), BF16),
        pltpu.VMEM((SEQS, 2, TOK, CH), BF16),
        dma((4,)),
        dma,
        dma,
        dma((GROUPS, N_TP - 1, GS)),
        dma((GROUPS, N_TP - 1, GS)),
        dma((GROUPS, N_TP - 1, GS)),
        dma((GROUPS, N_TP - 1, GS)),
        dma((GROUPS, N_SEQ - 1)),
        dma((GROUPS, N_SEQ - 1)),
        dma((GROUPS, N_SEQ - 1)),
        dma((GROUPS, N_SEQ - 1)),
        dma((SEQS, N_Y)),
        dma((SEQS, N_Y)),
        dma((SEQS, 2)),
        dma((SEQS, 2)),
        dma((SEQS, 4)),
        dma((SEQS, 4)),
    ]
    return pl.pallas_call(
        mix_kernel,
        out_shape=(
            jax.ShapeDtypeStruct((SEQS, TOK, CH), BF16),
            jax.ShapeDtypeStruct((1, SEQS, NS, CH), F32),
        ),
        in_specs=[vmem] * 10 + [anym] * 4,
        out_specs=(vmem, vmem),
        scratch_shapes=scratch,
        compiler_params=pltpu.CompilerParams(
            collective_id=0, has_side_effects=True, vmem_limit_bytes=62 * 1024 * 1024
        ),
    )(
        inner_x,
        conv_tail,
        conv_weight,
        conv_bias.reshape(1, CH),
        xproj_dt,
        xproj_bc,
        dt_bias.reshape(1, CH),
        decay_log,
        skip_gain.reshape(8, 128),
        init_state,
        inner_z,
        dt_weight,
        out_weight,
        residual,
    )


def solution(mesh):
    in_specs = (
        P(None, "seq", "tp"),
        P(None, "seq", "tp"),
        P(None, None, "tp"),
        P(None, "tp"),
        P("tp"),
        P("tp", None),
        P("tp", None),
        P(None, "tp"),
        P("tp"),
        P(None, "tp"),
        P("tp"),
        P("tp", None),
        P(None, "seq", "tp"),
        P(None, None, "tp"),
    )
    out_specs = (P(None, "seq", "tp"), P("seq", None, None, "tp"))
    return jax.shard_map(body, mesh=mesh, in_specs=in_specs, out_specs=out_specs, check_vma=False)
```

```python
import jax
import jax.numpy as jnp
from jax import lax
from jax.experimental import pallas as pl
from jax.experimental.pallas import tpu as pltpu
from jax.sharding import PartitionSpec as P

MESH = pl.DeviceIdType.MESH
F32 = jnp.float32
BF16 = jnp.bfloat16
LOG2E = 1.4426950408889634

N_SEQ = 16
N_TP = 8
N_X = 4
N_Y = 4
N_Z = 4
SEQS = 4
TOK = 128
CH = 1024
NG = CH // 128
RANK = 512
LOWW = RANK + 128
NS = 16
ROWS = SEQS * TOK
HALF = TOK // 2
OWN = HALF // N_Y
EXROWS = (NS + 2) * 8


def mix_kernel(
    tail_ref,
    cw_ref,
    cb_ref,
    xbc_ref,
    dtb_ref,
    decay_ref,
    skip_ref,
    x_hbm,
    xdt_hbm,
    init_hbm,
    dtw_hbm,
    z_hbm,
    w_hbm,
    res_hbm,
    out_ref,
    st_ref,
    x_ref,
    xdt_ref,
    init_ref,
    dtw_ref,
    z_ref,
    w_ref,
    res_ref,
    rim_out,
    rim_in,
    joined,
    act,
    xg,
    dtg,
    splat,
    pick,
    pre,
    rate_t,
    init_t,
    flip,
    lowp,
    lows,
    lowr,
    lown,
    exx,
    exz,
    before,
    since,
    ent,
    snd,
    rcv,
    opp,
    fin,
    load_sem,
    rim_sem,
    lsib_sem,
    low_sem,
    nrm_sem,
    nsib_sem,
    exx_sem,
    exz_sem,
    sib_sem,
    opp_sem,
    fin_sem,
):
    q = lax.axis_index("seq")
    t = lax.axis_index("tp")
    z, x = q // N_X, lax.rem(q, N_X)
    y, core = t // 2, lax.rem(t, 2)

    sib = (q, y * 2 + 1 - core)

    def at_y(k):
        return (q, lax.rem(y + k, N_Y) * 2 + core)

    def at_x(k):
        return (z * N_X + lax.rem(x + k, N_X), t)

    def at_z(k):
        return (lax.rem(z + k, N_Z) * N_X + x, t)

    up, down = at_y(1), at_y(3)
    after = (lax.rem(q + 1, N_SEQ), t)
    prior = (lax.rem(q + N_SEQ - 1, N_SEQ), t)

    def remote(src, dst, sems, dev):
        return pltpu.make_async_remote_copy(
            src_ref=src, dst_ref=dst, send_sem=sems.at[0], recv_sem=sems.at[1], device_id=dev, device_id_type=MESH
        )

    barrier = pltpu.get_barrier_semaphore()
    peers = [after, prior, sib] + [at_y(k) for k in (1, 2, 3)]
    peers += [at_x(k) for k in (1, 2, 3)] + [at_z(k) for k in (1, 2, 3)]
    loads = [
        pltpu.make_async_copy(src, dst, load_sem.at[i])
        for i, (src, dst) in enumerate(
            (
                (x_hbm, x_ref),
                (xdt_hbm, xdt_ref),
                (init_hbm, init_ref),
                (dtw_hbm, dtw_ref),
                (w_hbm, w_ref),
                (z_hbm, z_ref),
                (res_hbm, res_ref),
            )
        )
    ]
    x_load, xdt_load, init_load, dtw_load, w_load, z_load, res_load = loads
    x_load.start()
    for dev in peers:
        pl.semaphore_signal(barrier, inc=1, device_id=dev, device_id_type=MESH)
    for c in loads[1:]:
        c.start()

    x_load.wait()
    row8 = lax.broadcasted_iota(jnp.int32, (8, CH), 0)
    last = [x_ref[s, TOK - 16 : TOK, :].astype(F32)[8:16, :] for s in range(SEQS)]
    packed = [jnp.where(row8 < 4, pltpu.roll(last[s], 4, 0), last[s + 1]) for s in (0, 2)]
    rim_out[...] = jnp.concatenate(packed, axis=0).astype(BF16)

    pl.semaphore_wait(barrier, len(peers))
    rim = remote(rim_out, rim_in, rim_sem, after)
    rim.start()

    def conv_block(s, b):
        r = pl.multiple_of(b * 16, 16)
        window = joined[s, pl.ds(r, 24), :]
        mixed = cb_ref[...] + cw_ref[0:1, :] * window[5:21, :]
        for k in range(1, 4):
            mixed = mixed + cw_ref[k : k + 1, :] * window[5 + k : 21 + k, :]
        rounded = (mixed / (1.0 + jnp.exp(-mixed))).astype(BF16)
        act[pl.ds(pl.multiple_of(s * TOK + r, 16), 16), :] = rounded
        wide = rounded.astype(F32)
        for h in range(2):
            base = pl.multiple_of((s * (TOK // 8) + b * 2 + h) * 64, 64)
            for c in range(NG):
                xg[pl.ds(base + c * 8, 8), :] = wide[h * 8 : h * 8 + 8, c * 128 : (c + 1) * 128]

    @pl.loop(0, SEQS)
    def _(s):
        @pl.loop(0, TOK // 16)
        def _(b):
            r = pl.multiple_of(b * 16, 16)
            joined[s, pl.ds(r + 8, 16), :] = x_ref[s, pl.ds(r, 16), :].astype(F32)

        @pl.loop(1, TOK // 16)
        def _(b):
            conv_block(s, b)

    for nb in range(NS // 8):
        for c in range(NG):
            flip[c * 8 : (c + 1) * 8, :] = -jnp.exp(decay_ref[nb * 8 : nb * 8 + 8, c * 128 : (c + 1) * 128]) * LOG2E
        for i in range(8):
            rate_t[nb * 8 + i] = flip[pl.ds(i, 8, stride=8), :]

    init_load.wait()

    @pl.loop(0, SEQS)
    def _(s):
        for nb in range(NS // 8):
            for c in range(NG):
                flip[c * 8 : (c + 1) * 8, :] = init_ref[s, nb * 8 : nb * 8 + 8, c * 128 : (c + 1) * 128]
            for i in range(8):
                init_t[s, nb * 8 + i] = flip[pl.ds(i, 8, stride=8), :]

    for n in range(2 * NS):
        r = lax.broadcasted_iota(jnp.int32, (128, 128), 0)
        pick[:, n * 128 : (n + 1) * 128] = jnp.where((r == n) | (r == n + 2 * NS), 1.0, 0.0).astype(BF16)
    for s in range(SEQS):
        lowp[s, :, RANK:] = jnp.zeros((TOK, LOWW - RANK), BF16)

    half = pl.ds(pl.multiple_of(core * HALF, HALF), HALF)
    other = pl.ds(pl.multiple_of((1 - core) * HALF, HALF), HALF)
    mine = pl.ds(pl.multiple_of(core * HALF + y * OWN, OWN), OWN)

    def share(k):
        return pl.ds(pl.multiple_of(lax.rem(y + k, N_Y) * OWN, OWN), OWN)

    def lsib_copy(s):
        return remote(lowp.at[s, other], lows.at[s], lsib_sem.at[s], sib)

    def low_copy(s, k):
        return remote(lows.at[s, share(k)], lowr.at[s, k - 1], low_sem.at[s, k - 1], at_y(k))

    def nrm_copy(s, k):
        return remote(lown.at[s, mine], lown.at[s, mine], nrm_sem.at[s, k - 1], at_y(k))

    def nsib_copy(s):
        return remote(lown.at[s, half], lown.at[s, half], nsib_sem.at[s], sib)

    def exx_copy(s, k):
        return remote(exx.at[s, x], exx.at[s, x], exx_sem.at[s, k - 1], at_x(k))

    def exz_copy(s, k):
        return remote(exz.at[s, z], exz.at[s, z], exz_sem.at[s, k - 1], at_z(k))

    def low_partial(s):
        conv_block(s, 0)
        rows = act[s * TOK : (s + 1) * TOK, :]
        lowp[s, :, 0:RANK] = jnp.dot(rows, xdt_ref[...], preferred_element_type=F32).astype(BF16)
        lowp[s, :, RANK : RANK + 2 * NS] = lax.dot_general(
            rows, xbc_ref[...], (((1,), (1,)), ((), ())), preferred_element_type=F32
        ).astype(BF16)
        lsib_copy(s).start()

    def low_pair(s):
        lsib_copy(s).wait_recv()
        lows[s] = (lows[s].astype(F32) + lowp[s, half, :].astype(F32)).astype(BF16)
        for k in (2, 1, 3):
            low_copy(s, k).start()

    def normalise(s):
        total = lows[s, share(0), :].astype(F32)
        for k in range(1, N_Y):
            low_copy(s, k).wait_recv()
        for k in range(1, N_Y):
            total = total + lowr[s, k - 1].astype(F32)
        low = total[:, :RANK]
        scale = lax.rsqrt(jnp.mean(low * low, axis=-1, keepdims=True) + 1e-6)
        lown[s, mine, 0:RANK] = (low * scale).astype(BF16)
        bc = total[:, RANK:]
        high = bc.astype(BF16).astype(F32)
        lown[s, mine, RANK:] = (high + pltpu.roll(bc - high, 2 * NS, 1)).astype(BF16)
        for k in (2, 1, 3):
            nrm_copy(s, k).start()

    def low_forward(s):
        for k in range(1, N_Y):
            nrm_copy(s, k).wait_recv()
        nsib_copy(s).start()

    def steps(s):
        nsib_copy(s).wait_recv()
        if s == 0:
            dtw_load.wait()
        pre[...] = jnp.dot(lown[s, :, 0:RANK], dtw_ref[...], preferred_element_type=F32)

        @pl.loop(0, TOK // 16)
        def _(b):
            r = pl.multiple_of(b * 16, 16)
            v = pre[pl.ds(r, 16), :] + dtb_ref[...]
            dt = jnp.maximum(v, 0.0) + jnp.log1p(jnp.exp(-jnp.abs(v)))
            for h in range(2):
                base = pl.multiple_of((s * (TOK // 8) + b * 2 + h) * 64, 64)
                for c in range(NG):
                    dtg[pl.ds(base + c * 8, 8), :] = dt[h * 8 : h * 8 + 8, c * 128 : (c + 1) * 128]

        maps = lown[s, :, RANK:]
        for p in range(2 * NS // 8):
            wide = jnp.dot(maps, pick[:, p * 1024 : (p + 1) * 1024], preferred_element_type=F32)
            for i in range(8):
                at = (p * 8 + i) * ROWS + s * TOK
                splat[at : at + TOK, :] = wide[:, i * 128 : (i + 1) * 128]

    def put_states(dst, s, i, states, elapsed):
        for m in range(NS // 2):
            dst[s, i, m * 16 : (m + 1) * 16, :] = jnp.concatenate(states[2 * m : 2 * m + 2], axis=0).astype(BF16)
        high = elapsed.astype(BF16).astype(F32)
        dst[s, i, NS * 8 :, :] = jnp.concatenate([high, elapsed - high], axis=0).astype(BF16)

    def get_elapsed(src, s, i):
        parts = src[s, i, NS * 8 :, :].astype(F32)
        return parts[0:8] + parts[8:16]

    def first_pass(s):
        rates = [rate_t[n] for n in range(NS)]

        def block(b, carry):
            h, elapsed = list(carry[0]), carry[1]
            base = pl.multiple_of((s * (TOK // 8) + b) * 64, 64)
            for i in range(8):
                dt = dtg[pl.ds(base + i, 8, stride=8), :]
                u = dt * xg[pl.ds(base + i, 8, stride=8), :]
                elapsed = elapsed + dt
                tok = s * TOK + b * 8 + i
                for n in range(NS):
                    h[n] = jnp.exp2(rates[n] * dt) * h[n] + splat[pl.ds(n * ROWS + tok, 1), :] * u
            return (tuple(h), elapsed)

        zero = jnp.zeros((8, 128), F32)
        h, elapsed = lax.fori_loop(0, TOK // 8, block, ((zero,) * NS, zero))
        put_states(exx, s, x, h, elapsed)
        for k in (2, 1, 3):
            exx_copy(s, k).start()

    def along_x(s):
        for k in range(1, N_X):
            exx_copy(s, k).wait_recv()
        spans = [get_elapsed(exx, s, i) for i in range(N_X)]
        totals = []
        for m in range(NS // 2):
            pairs = [exx[s, i, m * 16 : (m + 1) * 16, :].astype(F32) for i in range(N_X)]
            for h in range(2):
                n = 2 * m + h
                state = pairs[0][h * 8 : h * 8 + 8]
                kept = jnp.where(x == 1, state, jnp.zeros_like(state))
                for i in range(1, N_X):
                    state = jnp.exp2(rate_t[n] * spans[i]) * state + pairs[i][h * 8 : h * 8 + 8]
                    if i < N_X - 1:
                        kept = jnp.where(x == i + 1, state, kept)
                before[s, n] = kept
                totals.append(state)
        span = spans[0]
        kept = jnp.where(x == 1, span, jnp.zeros_like(span))
        for i in range(1, N_X):
            span = span + spans[i]
            if i < N_X - 1:
                kept = jnp.where(x == i + 1, span, kept)
        since[s] = kept
        put_states(exz, s, z, totals, span)
        for k in (2, 1, 3):
            exz_copy(s, k).start()

    def along_z(s):
        for k in range(1, N_Z):
            exz_copy(s, k).wait_recv()
        spans = [get_elapsed(exz, s, i) for i in range(N_Z - 1)]
        last_span = since[s]
        for m in range(NS // 2):
            pairs = [exz[s, i, m * 16 : (m + 1) * 16, :].astype(F32) for i in range(N_Z - 1)]
            for h in range(2):
                n = 2 * m + h
                rate = rate_t[n]
                state = init_t[s, n]
                for i in range(N_Z - 1):
                    later = jnp.exp2(rate * spans[i]) * state + pairs[i][h * 8 : h * 8 + 8]
                    state = jnp.where(i < z, later, state)
                ent[s, n] = jnp.exp2(rate * last_span) * state + before[s, n]

    def second_pass(s):
        rates = [rate_t[n] for n in range(NS)]
        skip = skip_ref[...]

        def block(b, h):
            h = list(h)
            base = pl.multiple_of((s * (TOK // 8) + b) * 64, 64)
            for i in range(8):
                dt = dtg[pl.ds(base + i, 8, stride=8), :]
                v = xg[pl.ds(base + i, 8, stride=8), :]
                u = dt * v
                tok = s * TOK + b * 8 + i
                total = skip * v
                for n in range(NS):
                    h[n] = jnp.exp2(rates[n] * dt) * h[n] + splat[pl.ds(n * ROWS + tok, 1), :] * u
                    total = total + splat[pl.ds((NS + n) * ROWS + tok, 1), :] * h[n]
                xg[pl.ds(base + i, 8, stride=8), :] = total
            return tuple(h)

        h = lax.fori_loop(0, TOK // 8, block, tuple(ent[s, n] for n in range(NS)))
        for nb in range(NS // 8):
            for i in range(8):
                flip[pl.ds(i, 8, stride=8), :] = h[nb * 8 + i]
            for c in range(NG):
                st_ref[0, s, nb * 8 : nb * 8 + 8, c * 128 : (c + 1) * 128] = flip[c * 8 : (c + 1) * 8, :]

    def gate(s):
        @pl.loop(0, TOK // 16)
        def _(b):
            r = pl.multiple_of(b * 16, 16)
            v = z_ref[s, pl.ds(r, 16), :].astype(F32)
            sz = v / (1.0 + jnp.exp(-v))
            base = pl.multiple_of((s * (TOK // 8) + b * 2) * 64, 64)
            for c in range(NG):
                scanned = jnp.concatenate(
                    [xg[pl.ds(base + c * 8, 8), :], xg[pl.ds(base + 64 + c * 8, 8), :]], axis=0
                )
                act[pl.ds(pl.multiple_of(s * TOK + r, 16), 16), c * 128 : (c + 1) * 128] = (
                    scanned * sz[:, c * 128 : (c + 1) * 128]
                ).astype(BF16)

    def product(s, j, who):
        dest = lax.rem(y + j, N_Y) * 2 + who
        cols = pl.ds(pl.multiple_of(dest * CH, CH), CH)
        return jnp.dot(act[s * TOK : (s + 1) * TOK, :], w_ref[:, cols], preferred_element_type=F32)

    lo, hi = pl.ds(0, HALF), pl.ds(HALF, HALF)

    def sib_copy(s, j):
        return remote(snd.at[s, j], rcv.at[s, j], sib_sem.at[s, j], sib)

    def opp_up(s):
        return remote(rcv.at[s, 2, lo], opp.at[s, 0], opp_sem.at[s, 0], up)

    def opp_down(s):
        return remote(rcv.at[s, 2, hi], opp.at[s, 1], opp_sem.at[s, 1], down)

    def own_up(s):
        return remote(rcv.at[s, 1, hi], fin.at[s, 0, hi], fin_sem.at[s, 0], up)

    def own_down(s):
        return remote(rcv.at[s, 3, lo], fin.at[s, 1, lo], fin_sem.at[s, 1], down)

    def fwd_up(s):
        return remote(rcv.at[s, 1, lo], fin.at[s, 0, lo], fin_sem.at[s, 2], up)

    def fwd_down(s):
        return remote(rcv.at[s, 3, hi], fin.at[s, 1, hi], fin_sem.at[s, 3], down)

    def for_sibling(s, j):
        snd[s, j] = product(s, j, 1 - core).astype(BF16)
        sib_copy(s, j).start()

    def for_chip(s, j):
        part = product(s, j, core)
        sib_copy(s, j).wait_recv()
        rcv[s, j] = (part + rcv[s, j].astype(F32)).astype(BF16)
        if j == 2:
            opp_up(s).start()
            opp_down(s).start()
        if j == 1:
            own_up(s).start()
        if j == 3:
            own_down(s).start()

    def forward(s):
        for d in range(2):
            (opp_up(s) if d == 0 else opp_down(s)).wait_recv()
            j, r0 = (1, 0) if d == 0 else (3, HALF)

            @pl.loop(0, HALF // 16)
            def _(b):
                r = pl.multiple_of(b * 16, 16)
                part = rcv[s, j, pl.ds(r0 + r, 16), :].astype(F32)
                rcv[s, j, pl.ds(r0 + r, 16), :] = (part + opp[s, d, pl.ds(r, 16), :].astype(F32)).astype(BF16)

            (fwd_up(s) if d == 0 else fwd_down(s)).start()

    def finish(s):
        for c in (own_up(s), own_down(s), fwd_up(s), fwd_down(s)):
            c.wait_recv()

        @pl.loop(0, TOK // 16)
        def _(b):
            r = pl.ds(pl.multiple_of(b * 16, 16), 16)
            total = res_ref[s, r, :].astype(F32) + rcv[s, 0, r, :].astype(F32)
            total = total + fin[s, 0, r, :].astype(F32) + fin[s, 1, r, :].astype(F32)
            out_ref[s, r, :] = total.astype(BF16)

    def project(s):
        along_z(s)
        second_pass(s)
        if s == 0:
            z_load.wait()
        gate(s)
        if s == 0:
            w_load.wait()
        else:
            forward(s - 1)
        for_sibling(s, 2)
        for_sibling(s, 1)
        for_chip(s, 2)
        for_sibling(s, 3)
        for_chip(s, 1)
        for_sibling(s, 0)
        for_chip(s, 3)
        for_chip(s, 0)
        if s == 1:
            res_load.wait()
        if s > 1:
            finish(s - 2)

    rim.wait()
    for s in range(SEQS):
        part = rim_in[...].astype(F32)[(s // 2) * 8 : (s // 2) * 8 + 8, :]
        joined[s, 0:8, :] = pltpu.roll(part, 4, 0) if s % 2 == 0 else part

    @pl.when(q == 0)
    def _():
        for s in range(SEQS):
            joined[s, 5:8, :] = tail_ref[:, s, :].astype(F32)

    xdt_load.wait()
    for s in range(SEQS):
        low_partial(s)
        if s > 0:
            low_pair(s - 1)
    low_pair(SEQS - 1)
    for s in range(SEQS):
        normalise(s)
    low_forward(0)
    low_forward(1)
    steps(0)
    first_pass(0)
    low_forward(2)
    steps(1)
    first_pass(1)
    low_forward(3)
    along_x(0)
    steps(2)
    first_pass(2)
    along_x(1)
    project(0)
    steps(3)
    first_pass(3)
    along_x(2)
    project(1)
    along_x(3)
    project(2)
    project(3)
    forward(3)
    finish(2)
    finish(3)

    for s in range(SEQS):
        lsib_copy(s).wait_send()
        nsib_copy(s).wait_send()
        for k in range(1, N_Y):
            low_copy(s, k).wait_send()
            nrm_copy(s, k).wait_send()
            exx_copy(s, k).wait_send()
            exz_copy(s, k).wait_send()
        for j in range(N_Y):
            sib_copy(s, j).wait_send()
        for c in (opp_up(s), opp_down(s), own_up(s), own_down(s), fwd_up(s), fwd_down(s)):
            c.wait_send()


def place_kernel(out_src, st_src, out_dst, st_dst, out_buf, st_buf, sem):
    arrive, leave = [], []
    for s in range(SEQS):
        arrive.append(pltpu.make_async_copy(out_src.at[s], out_buf.at[s], sem.at[0, s]))
        leave.append(pltpu.make_async_copy(out_buf.at[s], out_dst.at[s], sem.at[1, s]))
    arrive.append(pltpu.make_async_copy(st_src, st_buf, sem.at[0, SEQS]))
    leave.append(pltpu.make_async_copy(st_buf, st_dst, sem.at[1, SEQS]))
    for c in arrive:
        c.start()
    for a, c in zip(arrive, leave):
        a.wait()
        c.start()
    for c in leave:
        c.wait()


def place(out, st):
    anym = pl.BlockSpec(memory_space=pl.ANY)
    return pl.pallas_call(
        place_kernel,
        out_shape=(jax.ShapeDtypeStruct(out.shape, out.dtype), jax.ShapeDtypeStruct(st.shape, st.dtype)),
        in_specs=[anym, anym],
        out_specs=(anym, anym),
        scratch_shapes=[
            pltpu.VMEM(out.shape, out.dtype),
            pltpu.VMEM(st.shape, st.dtype),
            pltpu.SemaphoreType.DMA((2, SEQS + 1)),
        ],
    )(out, st)


def body(
    inner_x,
    inner_z,
    conv_tail,
    conv_weight,
    conv_bias,
    xproj_dt,
    xproj_bc,
    dt_weight,
    dt_bias,
    decay_log,
    skip_gain,
    out_weight,
    residual,
    init_state,
):
    vmem = pl.BlockSpec(memory_space=pltpu.VMEM)
    anym = pl.BlockSpec(memory_space=pl.ANY)
    dma = pltpu.SemaphoreType.DMA
    scratch = [
        pltpu.VMEM((SEQS, TOK, CH), BF16),
        pltpu.VMEM((CH, RANK), BF16),
        pltpu.VMEM((SEQS, NS, CH), F32),
        pltpu.VMEM((RANK, CH), BF16),
        pltpu.VMEM((SEQS, TOK, CH), BF16),
        pltpu.VMEM((CH, N_TP * CH), BF16),
        pltpu.VMEM((SEQS, TOK, CH), BF16),
        pltpu.VMEM((16, CH), BF16),
        pltpu.VMEM((16, CH), BF16),
        pltpu.VMEM((SEQS, TOK + 8, CH), F32),
        pltpu.VMEM((ROWS, CH), BF16),
        pltpu.VMEM((ROWS * 8, 128), F32),
        pltpu.VMEM((ROWS * 8, 128), F32),
        pltpu.VMEM((2 * NS * ROWS, 128), F32),
        pltpu.VMEM((128, 2 * NS * 128), BF16),
        pltpu.VMEM((TOK, CH), F32),
        pltpu.VMEM((NS, 8, 128), F32),
        pltpu.VMEM((SEQS, NS, 8, 128), F32),
        pltpu.VMEM((64, 128), F32),
        pltpu.VMEM((SEQS, TOK, LOWW), BF16),
        pltpu.VMEM((SEQS, HALF, LOWW), BF16),
        pltpu.VMEM((SEQS, N_Y - 1, OWN, LOWW), BF16),
        pltpu.VMEM((SEQS, TOK, LOWW), BF16),
        pltpu.VMEM((SEQS, N_X, EXROWS, 128), BF16),
        pltpu.VMEM((SEQS, N_Z, EXROWS, 128), BF16),
        pltpu.VMEM((SEQS, NS, 8, 128), F32),
        pltpu.VMEM((SEQS, 8, 128), F32),
        pltpu.VMEM((SEQS, NS, 8, 128), F32),
        pltpu.VMEM((SEQS, N_Y, TOK, CH), BF16),
        pltpu.VMEM((SEQS, N_Y, TOK, CH), BF16),
        pltpu.VMEM((SEQS, 2, HALF, CH), BF16),
        pltpu.VMEM((SEQS, 2, TOK, CH), BF16),
        dma((7,)),
        dma((2,)),
        dma((SEQS, 2)),
        dma((SEQS, N_Y - 1, 2)),
        dma((SEQS, N_Y - 1, 2)),
        dma((SEQS, 2)),
        dma((SEQS, N_X - 1, 2)),
        dma((SEQS, N_Z - 1, 2)),
        dma((SEQS, N_Y, 2)),
        dma((SEQS, 2, 2)),
        dma((SEQS, 4, 2)),
    ]
    out, st = pl.pallas_call(
        mix_kernel,
        out_shape=(
            jax.ShapeDtypeStruct((SEQS, TOK, CH), BF16),
            jax.ShapeDtypeStruct((1, SEQS, NS, CH), F32),
        ),
        in_specs=[vmem] * 7 + [anym] * 7,
        out_specs=(vmem, vmem),
        scratch_shapes=scratch,
        compiler_params=pltpu.CompilerParams(
            collective_id=0, has_side_effects=True, vmem_limit_bytes=62 * 1024 * 1024
        ),
    )(
        jnp.transpose(conv_tail, (1, 0, 2)),
        conv_weight,
        conv_bias.reshape(1, CH),
        xproj_bc.T,
        dt_bias.reshape(1, CH),
        decay_log,
        skip_gain.reshape(8, 128),
        inner_x,
        xproj_dt,
        init_state,
        dt_weight,
        inner_z,
        out_weight,
        residual,
    )
    return place(out, st)


def solution(mesh):
    in_specs = (
        P(None, "seq", "tp"),
        P(None, "seq", "tp"),
        P(None, None, "tp"),
        P(None, "tp"),
        P("tp"),
        P("tp", None),
        P("tp", None),
        P(None, "tp"),
        P("tp"),
        P(None, "tp"),
        P("tp"),
        P("tp", None),
        P(None, "seq", "tp"),
        P(None, None, "tp"),
    )
    out_specs = (P(None, "seq", "tp"), P("seq", None, None, "tp"))
    return jax.shard_map(body, mesh=mesh, in_specs=in_specs, out_specs=out_specs, check_vma=False)
```

```python
import jax
import jax.numpy as jnp
from jax import lax
from jax.experimental import pallas as pl
from jax.experimental.pallas import tpu as pltpu
from jax.sharding import PartitionSpec as P

MESH = pl.DeviceIdType.MESH
F32 = jnp.float32
BF16 = jnp.bfloat16
LOG2E = 1.4426950408889634

N_SEQ = 16
N_TP = 8
N_X = 4
N_Y = 4
N_Z = 4
SEQS = 4
TOK = 128
CH = 1024
NG = CH // 128
RANK = 512
LOWW = RANK + 128
NS = 16
ROWS = SEQS * TOK
HALF = TOK // 2
OWN = HALF // N_Y
EXROWS = (NS + 2) * 8


def mix_kernel(
    tail_hbm,
    cw_hbm,
    cb_hbm,
    xbc_hbm,
    dtb_hbm,
    decay_hbm,
    skip_hbm,
    x_hbm,
    xdt_hbm,
    init_hbm,
    dtw_hbm,
    z_hbm,
    w_hbm,
    res_hbm,
    out_ref,
    st_ref,
    tail_ref,
    cw_ref,
    cb_ref,
    xbc_ref,
    dtb_ref,
    decay_ref,
    skip_ref,
    x_ref,
    xdt_ref,
    init_ref,
    dtw_ref,
    z_ref,
    w_ref,
    res_ref,
    rim_out,
    rim_in,
    joined,
    act,
    xg,
    dtg,
    splat,
    pick,
    pre,
    rate_t,
    init_t,
    flip,
    lowp,
    lows,
    lowr,
    lown,
    exx,
    exz,
    before,
    since,
    ent,
    both,
    part,
    opp,
    fin,
    load_sem,
    rim_sem,
    lsib_sem,
    low_sem,
    nrm_sem,
    nsib_sem,
    exx_sem,
    exz_sem,
    wown_sem,
    wsib_sem,
    both_sem,
    opp_sem,
    fin_sem,
):
    q = lax.axis_index("seq")
    t = lax.axis_index("tp")
    z, x = q // N_X, lax.rem(q, N_X)
    y, core = t // 2, lax.rem(t, 2)

    sib = (q, y * 2 + 1 - core)

    def at_y(k):
        return (q, lax.rem(y + k, N_Y) * 2 + core)

    def at_x(k):
        return (z * N_X + lax.rem(x + k, N_X), t)

    def at_z(k):
        return (lax.rem(z + k, N_Z) * N_X + x, t)

    up, down = at_y(1), at_y(3)
    after = (lax.rem(q + 1, N_SEQ), t)
    prior = (lax.rem(q + N_SEQ - 1, N_SEQ), t)

    def remote(src, dst, sems, dev):
        return pltpu.make_async_remote_copy(
            src_ref=src, dst_ref=dst, send_sem=sems.at[0], recv_sem=sems.at[1], device_id=dev, device_id_type=MESH
        )

    barrier = pltpu.get_barrier_semaphore()
    peers = [after, prior, sib] + [at_y(k) for k in (1, 2, 3)]
    peers += [at_x(k) for k in (1, 2, 3)] + [at_z(k) for k in (1, 2, 3)]
    loads = [
        pltpu.make_async_copy(src, dst, load_sem.at[i])
        for i, (src, dst) in enumerate(
            (
                (x_hbm, x_ref),
                (cw_hbm, cw_ref),
                (cb_hbm, cb_ref),
                (tail_hbm, tail_ref),
                (xdt_hbm, xdt_ref),
                (xbc_hbm, xbc_ref),
                (decay_hbm, decay_ref),
                (dtb_hbm, dtb_ref),
                (skip_hbm, skip_ref),
                (dtw_hbm, dtw_ref),
                (init_hbm, init_ref),
                (z_hbm, z_ref),
                (res_hbm, res_ref),
            )
        )
    ]

    own_rows = pl.ds(pl.multiple_of(core * CH, CH), CH)

    def w_block(j):
        return pl.ds(pl.multiple_of(lax.rem(y + j, N_Y) * CH, CH), CH)

    def w_source(j, who):
        return w_hbm.at[:, pl.ds(pl.multiple_of((lax.rem(y + j, N_Y) * 2 + who) * CH, CH), CH)]

    def w_own(j):
        return pltpu.make_async_copy(w_source(j, core), w_ref.at[own_rows, w_block(j)], wown_sem.at[j])

    def w_give(j):
        return remote(w_source(j, 1 - core), w_ref.at[own_rows, w_block(j)], wsib_sem.at[j], sib)

    loads[0].start()
    for dev in peers:
        pl.semaphore_signal(barrier, inc=1, device_id=dev, device_id_type=MESH)
    for c in loads[1:]:
        c.start()
    for j in (2, 1, 3, 0):
        w_own(j).start()

    loads[0].wait()
    row8 = lax.broadcasted_iota(jnp.int32, (8, CH), 0)
    last = [x_ref[s, TOK - 16 : TOK, :].astype(F32)[8:16, :] for s in range(SEQS)]
    packed = [jnp.where(row8 < 4, pltpu.roll(last[s], 4, 0), last[s + 1]) for s in (0, 2)]
    rim_out[...] = jnp.concatenate(packed, axis=0).astype(BF16)

    pl.semaphore_wait(barrier, len(peers))
    rim = remote(rim_out, rim_in, rim_sem, after)
    rim.start()
    w_give(2).start()

    def conv_block(s, b):
        r = pl.multiple_of(b * 16, 16)
        window = joined[s, pl.ds(r, 24), :]
        mixed = cb_ref[...] + cw_ref[0:1, :] * window[5:21, :]
        for k in range(1, 4):
            mixed = mixed + cw_ref[k : k + 1, :] * window[5 + k : 21 + k, :]
        rounded = (mixed / (1.0 + jnp.exp(-mixed))).astype(BF16)
        act[pl.ds(pl.multiple_of(s * TOK + r, 16), 16), :] = rounded
        wide = rounded.astype(F32)
        for h in range(2):
            base = pl.multiple_of((s * (TOK // 8) + b * 2 + h) * 64, 64)
            for c in range(NG):
                xg[pl.ds(base + c * 8, 8), :] = wide[h * 8 : h * 8 + 8, c * 128 : (c + 1) * 128]

    loads[1].wait()
    loads[2].wait()

    @pl.loop(0, SEQS)
    def _(s):
        @pl.loop(0, TOK // 16)
        def _(b):
            r = pl.multiple_of(b * 16, 16)
            joined[s, pl.ds(r + 8, 16), :] = x_ref[s, pl.ds(r, 16), :].astype(F32)

        @pl.loop(1, TOK // 16)
        def _(b):
            conv_block(s, b)

    for s in range(SEQS):
        lowp[s, :, RANK:] = jnp.zeros((TOK, LOWW - RANK), BF16)

    half = pl.ds(pl.multiple_of(core * HALF, HALF), HALF)
    other = pl.ds(pl.multiple_of((1 - core) * HALF, HALF), HALF)
    mine = pl.ds(pl.multiple_of(core * HALF + y * OWN, OWN), OWN)

    def share(k):
        return pl.ds(pl.multiple_of(lax.rem(y + k, N_Y) * OWN, OWN), OWN)

    def lsib_copy(s):
        return remote(lowp.at[s, other], lows.at[s], lsib_sem.at[s], sib)

    def low_copy(s, k):
        return remote(lows.at[s, share(k)], lowr.at[s, k - 1], low_sem.at[s, k - 1], at_y(k))

    def nrm_copy(s, k):
        return remote(lown.at[s, mine], lown.at[s, mine], nrm_sem.at[s, k - 1], at_y(k))

    def nsib_copy(s):
        return remote(lown.at[s, half], lown.at[s, half], nsib_sem.at[s], sib)

    def exx_copy(s, k):
        return remote(exx.at[s, x], exx.at[s, x], exx_sem.at[s, k - 1], at_x(k))

    def exz_copy(s, k):
        return remote(exz.at[s, z], exz.at[s, z], exz_sem.at[s, k - 1], at_z(k))

    def low_partial(s):
        conv_block(s, 0)
        rows = act[s * TOK : (s + 1) * TOK, :]
        lowp[s, :, 0:RANK] = jnp.dot(rows, xdt_ref[...], preferred_element_type=F32).astype(BF16)
        lowp[s, :, RANK : RANK + 2 * NS] = lax.dot_general(
            rows, xbc_ref[...], (((1,), (1,)), ((), ())), preferred_element_type=F32
        ).astype(BF16)
        lsib_copy(s).start()

    def low_pair(s):
        lsib_copy(s).wait_recv()
        lows[s] = (lows[s].astype(F32) + lowp[s, half, :].astype(F32)).astype(BF16)
        for k in (2, 1, 3):
            low_copy(s, k).start()

    def normalise(s):
        total = lows[s, share(0), :].astype(F32)
        for k in range(1, N_Y):
            low_copy(s, k).wait_recv()
        for k in range(1, N_Y):
            total = total + lowr[s, k - 1].astype(F32)
        low = total[:, :RANK]
        scale = lax.rsqrt(jnp.mean(low * low, axis=-1, keepdims=True) + 1e-6)
        lown[s, mine, 0:RANK] = (low * scale).astype(BF16)
        bc = total[:, RANK:]
        high = bc.astype(BF16).astype(F32)
        lown[s, mine, RANK:] = (high + pltpu.roll(bc - high, 2 * NS, 1)).astype(BF16)
        for k in (2, 1, 3):
            nrm_copy(s, k).start()

    def low_forward(s):
        for k in range(1, N_Y):
            nrm_copy(s, k).wait_recv()
        nsib_copy(s).start()

    def steps(s):
        nsib_copy(s).wait_recv()
        if s == 0:
            loads[9].wait()
        pre[...] = jnp.dot(lown[s, :, 0:RANK], dtw_ref[...], preferred_element_type=F32)

        @pl.loop(0, TOK // 16)
        def _(b):
            r = pl.multiple_of(b * 16, 16)
            v = pre[pl.ds(r, 16), :] + dtb_ref[...]
            dt = jnp.maximum(v, 0.0) + jnp.log1p(jnp.exp(-jnp.abs(v)))
            for h in range(2):
                base = pl.multiple_of((s * (TOK // 8) + b * 2 + h) * 64, 64)
                for c in range(NG):
                    dtg[pl.ds(base + c * 8, 8), :] = dt[h * 8 : h * 8 + 8, c * 128 : (c + 1) * 128]

        maps = lown[s, :, RANK:]
        for p in range(2 * NS // 8):
            wide = jnp.dot(maps, pick[:, p * 1024 : (p + 1) * 1024], preferred_element_type=F32)
            for i in range(8):
                at = (p * 8 + i) * ROWS + s * TOK
                splat[at : at + TOK, :] = wide[:, i * 128 : (i + 1) * 128]

    def put_states(dst, s, i, states, elapsed):
        for m in range(NS // 2):
            dst[s, i, m * 16 : (m + 1) * 16, :] = jnp.concatenate(states[2 * m : 2 * m + 2], axis=0).astype(BF16)
        high = elapsed.astype(BF16).astype(F32)
        dst[s, i, NS * 8 :, :] = jnp.concatenate([high, elapsed - high], axis=0).astype(BF16)

    def get_elapsed(src, s, i):
        parts = src[s, i, NS * 8 :, :].astype(F32)
        return parts[0:8] + parts[8:16]

    def first_pass(s):
        rates = [rate_t[n] for n in range(NS)]

        def block(b, carry):
            h, elapsed = list(carry[0]), carry[1]
            base = pl.multiple_of((s * (TOK // 8) + b) * 64, 64)
            for i in range(8):
                dt = dtg[pl.ds(base + i, 8, stride=8), :]
                u = dt * xg[pl.ds(base + i, 8, stride=8), :]
                elapsed = elapsed + dt
                tok = s * TOK + b * 8 + i
                for n in range(NS):
                    h[n] = jnp.exp2(rates[n] * dt) * h[n] + splat[pl.ds(n * ROWS + tok, 1), :] * u
            return (tuple(h), elapsed)

        zero = jnp.zeros((8, 128), F32)
        h, elapsed = lax.fori_loop(0, TOK // 8, block, ((zero,) * NS, zero))
        put_states(exx, s, x, h, elapsed)
        for k in (2, 1, 3):
            exx_copy(s, k).start()

    def along_x(s):
        for k in range(1, N_X):
            exx_copy(s, k).wait_recv()
        spans = [get_elapsed(exx, s, i) for i in range(N_X)]
        totals = []
        for m in range(NS // 2):
            pairs = [exx[s, i, m * 16 : (m + 1) * 16, :].astype(F32) for i in range(N_X)]
            for h in range(2):
                n = 2 * m + h
                state = pairs[0][h * 8 : h * 8 + 8]
                kept = jnp.where(x == 1, state, jnp.zeros_like(state))
                for i in range(1, N_X):
                    state = jnp.exp2(rate_t[n] * spans[i]) * state + pairs[i][h * 8 : h * 8 + 8]
                    if i < N_X - 1:
                        kept = jnp.where(x == i + 1, state, kept)
                before[s, n] = kept
                totals.append(state)
        span = spans[0]
        kept = jnp.where(x == 1, span, jnp.zeros_like(span))
        for i in range(1, N_X):
            span = span + spans[i]
            if i < N_X - 1:
                kept = jnp.where(x == i + 1, span, kept)
        since[s] = kept
        put_states(exz, s, z, totals, span)
        for k in (2, 1, 3):
            exz_copy(s, k).start()

    def along_z(s):
        for k in range(1, N_Z):
            exz_copy(s, k).wait_recv()
        spans = [get_elapsed(exz, s, i) for i in range(N_Z - 1)]
        last_span = since[s]
        for m in range(NS // 2):
            pairs = [exz[s, i, m * 16 : (m + 1) * 16, :].astype(F32) for i in range(N_Z - 1)]
            for h in range(2):
                n = 2 * m + h
                rate = rate_t[n]
                state = init_t[s, n]
                for i in range(N_Z - 1):
                    later = jnp.exp2(rate * spans[i]) * state + pairs[i][h * 8 : h * 8 + 8]
                    state = jnp.where(i < z, later, state)
                ent[s, n] = jnp.exp2(rate * last_span) * state + before[s, n]

    def second_pass(s):
        rates = [rate_t[n] for n in range(NS)]
        skip = skip_ref[...]

        def block(b, h):
            h = list(h)
            base = pl.multiple_of((s * (TOK // 8) + b) * 64, 64)
            for i in range(8):
                dt = dtg[pl.ds(base + i, 8, stride=8), :]
                v = xg[pl.ds(base + i, 8, stride=8), :]
                u = dt * v
                tok = s * TOK + b * 8 + i
                total = skip * v
                for n in range(NS):
                    h[n] = jnp.exp2(rates[n] * dt) * h[n] + splat[pl.ds(n * ROWS + tok, 1), :] * u
                    total = total + splat[pl.ds((NS + n) * ROWS + tok, 1), :] * h[n]
                xg[pl.ds(base + i, 8, stride=8), :] = total
            return tuple(h)

        h = lax.fori_loop(0, TOK // 8, block, tuple(ent[s, n] for n in range(NS)))
        for nb in range(NS // 8):
            for i in range(8):
                flip[pl.ds(i, 8, stride=8), :] = h[nb * 8 + i]
            for c in range(NG):
                st_ref[0, s, nb * 8 : nb * 8 + 8, c * 128 : (c + 1) * 128] = flip[c * 8 : (c + 1) * 8, :]

    def gate(s):
        @pl.loop(0, TOK // 16)
        def _(b):
            r = pl.multiple_of(b * 16, 16)
            v = z_ref[s, pl.ds(r, 16), :].astype(F32)
            sz = v / (1.0 + jnp.exp(-v))
            base = pl.multiple_of((s * (TOK // 8) + b * 2) * 64, 64)
            for c in range(NG):
                scanned = jnp.concatenate(
                    [xg[pl.ds(base + c * 8, 8), :], xg[pl.ds(base + 64 + c * 8, 8), :]], axis=0
                )
                both[s, pl.ds(r, 16), pl.ds(pl.multiple_of(core * CH + c * 128, 128), 128)] = (
                    scanned * sz[:, c * 128 : (c + 1) * 128]
                ).astype(BF16)

    lo, hi = pl.ds(0, HALF), pl.ds(HALF, HALF)

    def both_copy(s):
        return remote(both.at[s, :, own_rows], both.at[s, :, own_rows], both_sem.at[s], sib)

    def opp_up(s):
        return remote(part.at[s, 2, lo], opp.at[s, 0], opp_sem.at[s, 0], up)

    def opp_down(s):
        return remote(part.at[s, 2, hi], opp.at[s, 1], opp_sem.at[s, 1], down)

    def own_up(s):
        return remote(part.at[s, 1, hi], fin.at[s, 0, hi], fin_sem.at[s, 0], up)

    def own_down(s):
        return remote(part.at[s, 3, lo], fin.at[s, 1, lo], fin_sem.at[s, 1], down)

    def fwd_up(s):
        return remote(part.at[s, 1, lo], fin.at[s, 0, lo], fin_sem.at[s, 2], up)

    def fwd_down(s):
        return remote(part.at[s, 3, hi], fin.at[s, 1, hi], fin_sem.at[s, 3], down)

    def for_chip(s, j):
        if s == 0:
            w_own(j).wait()
            w_give(j).wait_recv()
        part[s, j] = jnp.dot(both[s], w_ref[:, w_block(j)], preferred_element_type=F32).astype(BF16)
        if j == 2:
            opp_up(s).start()
            opp_down(s).start()
        if j == 1:
            own_up(s).start()
        if j == 3:
            own_down(s).start()

    def forward(s):
        for d in range(2):
            (opp_up(s) if d == 0 else opp_down(s)).wait_recv()
            j, r0 = (1, 0) if d == 0 else (3, HALF)

            @pl.loop(0, HALF // 16)
            def _(b):
                r = pl.multiple_of(b * 16, 16)
                here = part[s, j, pl.ds(r0 + r, 16), :].astype(F32)
                part[s, j, pl.ds(r0 + r, 16), :] = (here + opp[s, d, pl.ds(r, 16), :].astype(F32)).astype(BF16)

            (fwd_up(s) if d == 0 else fwd_down(s)).start()

    def finish(s):
        for c in (own_up(s), own_down(s), fwd_up(s), fwd_down(s)):
            c.wait_recv()

        @pl.loop(0, TOK // 16)
        def _(b):
            r = pl.ds(pl.multiple_of(b * 16, 16), 16)
            total = res_ref[s, r, :].astype(F32) + part[s, 0, r, :].astype(F32)
            total = total + fin[s, 0, r, :].astype(F32) + fin[s, 1, r, :].astype(F32)
            out_ref[s, r, :] = total.astype(BF16)

    def project(s):
        along_z(s)
        second_pass(s)
        if s == 0:
            loads[11].wait()
        gate(s)
        both_copy(s).start()

    def combine(s):
        both_copy(s).wait_recv()
        for j in (2, 1, 3, 0):
            for_chip(s, j)

    loads[3].wait()
    rim.wait()
    for s in range(SEQS):
        rows = rim_in[...].astype(F32)[(s // 2) * 8 : (s // 2) * 8 + 8, :]
        joined[s, 0:8, :] = pltpu.roll(rows, 4, 0) if s % 2 == 0 else rows

    @pl.when(q == 0)
    def _():
        for s in range(SEQS):
            joined[s, 5:8, :] = tail_ref[:, s, :].astype(F32)

    loads[4].wait()
    loads[5].wait()
    for s in range(SEQS):
        low_partial(s)
        if s > 0:
            low_pair(s - 1)
    low_pair(SEQS - 1)
    w_give(1).start()
    for s in range(SEQS):
        normalise(s)

    for i in (6, 7, 8):
        loads[i].wait()

    for nb in range(NS // 8):
        for c in range(NG):
            flip[c * 8 : (c + 1) * 8, :] = -jnp.exp(decay_ref[nb * 8 : nb * 8 + 8, c * 128 : (c + 1) * 128]) * LOG2E
        for i in range(8):
            rate_t[nb * 8 + i] = flip[pl.ds(i, 8, stride=8), :]

    for n in range(2 * NS):
        r = lax.broadcasted_iota(jnp.int32, (128, 128), 0)
        pick[:, n * 128 : (n + 1) * 128] = jnp.where((r == n) | (r == n + 2 * NS), 1.0, 0.0).astype(BF16)

    low_forward(0)
    w_give(3).start()
    low_forward(1)
    steps(0)
    first_pass(0)
    w_give(0).start()

    loads[10].wait()

    @pl.loop(0, SEQS)
    def _(s):
        for nb in range(NS // 8):
            for c in range(NG):
                flip[c * 8 : (c + 1) * 8, :] = init_ref[s, nb * 8 : nb * 8 + 8, c * 128 : (c + 1) * 128]
            for i in range(8):
                init_t[s, nb * 8 + i] = flip[pl.ds(i, 8, stride=8), :]

    low_forward(2)
    steps(1)
    first_pass(1)
    low_forward(3)
    along_x(0)
    steps(2)
    first_pass(2)
    along_x(1)
    project(0)
    steps(3)
    combine(0)
    along_x(2)
    project(1)
    forward(0)
    combine(1)
    first_pass(3)
    project(2)
    loads[12].wait()
    forward(1)
    along_x(3)
    combine(2)
    finish(0)
    project(3)
    forward(2)
    combine(3)
    finish(1)
    finish(2)
    forward(3)
    finish(3)

    for j in range(N_Y):
        w_give(j).wait_send()
    for s in range(SEQS):
        lsib_copy(s).wait_send()
        nsib_copy(s).wait_send()
        for k in range(1, N_Y):
            low_copy(s, k).wait_send()
            nrm_copy(s, k).wait_send()
            exx_copy(s, k).wait_send()
            exz_copy(s, k).wait_send()
        both_copy(s).wait_send()
        for c in (opp_up(s), opp_down(s), own_up(s), own_down(s), fwd_up(s), fwd_down(s)):
            c.wait_send()


def body(
    inner_x,
    inner_z,
    conv_tail,
    conv_weight,
    conv_bias,
    xproj_dt,
    xproj_bc,
    dt_weight,
    dt_bias,
    decay_log,
    skip_gain,
    out_weight,
    residual,
    init_state,
):
    vmem = pl.BlockSpec(memory_space=pltpu.VMEM)
    anym = pl.BlockSpec(memory_space=pl.ANY)
    dma = pltpu.SemaphoreType.DMA
    scratch = [
        pltpu.VMEM((3, SEQS, CH), BF16),
        pltpu.VMEM((4, CH), F32),
        pltpu.VMEM((1, CH), F32),
        pltpu.VMEM((2 * NS, CH), BF16),
        pltpu.VMEM((1, CH), F32),
        pltpu.VMEM((NS, CH), F32),
        pltpu.VMEM((8, 128), F32),
        pltpu.VMEM((SEQS, TOK, CH), BF16),
        pltpu.VMEM((CH, RANK), BF16),
        pltpu.VMEM((SEQS, NS, CH), F32),
        pltpu.VMEM((RANK, CH), BF16),
        pltpu.VMEM((SEQS, TOK, CH), BF16),
        pltpu.VMEM((2 * CH, N_Y * CH), BF16),
        pltpu.VMEM((SEQS, TOK, CH), BF16),
        pltpu.VMEM((16, CH), BF16),
        pltpu.VMEM((16, CH), BF16),
        pltpu.VMEM((SEQS, TOK + 8, CH), F32),
        pltpu.VMEM((ROWS, CH), BF16),
        pltpu.VMEM((ROWS * 8, 128), F32),
        pltpu.VMEM((ROWS * 8, 128), F32),
        pltpu.VMEM((2 * NS * ROWS, 128), F32),
        pltpu.VMEM((128, 2 * NS * 128), BF16),
        pltpu.VMEM((TOK, CH), F32),
        pltpu.VMEM((NS, 8, 128), F32),
        pltpu.VMEM((SEQS, NS, 8, 128), F32),
        pltpu.VMEM((64, 128), F32),
        pltpu.VMEM((SEQS, TOK, LOWW), BF16),
        pltpu.VMEM((SEQS, HALF, LOWW), BF16),
        pltpu.VMEM((SEQS, N_Y - 1, OWN, LOWW), BF16),
        pltpu.VMEM((SEQS, TOK, LOWW), BF16),
        pltpu.VMEM((SEQS, N_X, EXROWS, 128), BF16),
        pltpu.VMEM((SEQS, N_Z, EXROWS, 128), BF16),
        pltpu.VMEM((SEQS, NS, 8, 128), F32),
        pltpu.VMEM((SEQS, 8, 128), F32),
        pltpu.VMEM((SEQS, NS, 8, 128), F32),
        pltpu.VMEM((SEQS, TOK, 2 * CH), BF16),
        pltpu.VMEM((SEQS, N_Y, TOK, CH), BF16),
        pltpu.VMEM((SEQS, 2, HALF, CH), BF16),
        pltpu.VMEM((SEQS, 2, TOK, CH), BF16),
        dma((13,)),
        dma((2,)),
        dma((SEQS, 2)),
        dma((SEQS, N_Y - 1, 2)),
        dma((SEQS, N_Y - 1, 2)),
        dma((SEQS, 2)),
        dma((SEQS, N_X - 1, 2)),
        dma((SEQS, N_Z - 1, 2)),
        dma((N_Y,)),
        dma((N_Y, 2)),
        dma((SEQS, 2)),
        dma((SEQS, 2, 2)),
        dma((SEQS, 4, 2)),
    ]
    out, st = pl.pallas_call(
        mix_kernel,
        out_shape=(
            pltpu.VMEM((SEQS, TOK, CH), BF16),
            pltpu.VMEM((1, SEQS, NS, CH), F32),
        ),
        in_specs=[anym] * 14,
        out_specs=(vmem, vmem),
        scratch_shapes=scratch,
        compiler_params=pltpu.CompilerParams(
            collective_id=0, has_side_effects=True, vmem_limit_bytes=62 * 1024 * 1024
        ),
    )(
        jnp.transpose(conv_tail, (1, 0, 2)),
        conv_weight,
        conv_bias.reshape(1, CH),
        xproj_bc.T,
        dt_bias.reshape(1, CH),
        decay_log,
        skip_gain.reshape(8, 128),
        inner_x,
        xproj_dt,
        init_state,
        dt_weight,
        inner_z,
        out_weight,
        residual,
    )
    return out, st


def solution(mesh):
    in_specs = (
        P(None, "seq", "tp"),
        P(None, "seq", "tp"),
        P(None, None, "tp"),
        P(None, "tp"),
        P("tp"),
        P("tp", None),
        P("tp", None),
        P(None, "tp"),
        P("tp"),
        P(None, "tp"),
        P("tp"),
        P("tp", None),
        P(None, "seq", "tp"),
        P(None, None, "tp"),
    )
    out_specs = (P(None, "seq", "tp"), P("seq", None, None, "tp"))
    return jax.shard_map(body, mesh=mesh, in_specs=in_specs, out_specs=out_specs, check_vma=False)
```

```python
import jax
import jax.numpy as jnp
from jax import lax
from jax.experimental import pallas as pl
from jax.experimental.pallas import tpu as pltpu
from jax.sharding import PartitionSpec as P

MESH = pl.DeviceIdType.MESH
F32 = jnp.float32
BF16 = jnp.bfloat16
LOG2E = 1.4426950408889634

N_SEQ = 16
N_TP = 8
N_X = 4
N_Y = 4
N_Z = 4
SEQS = 4
TOK = 128
CH = 1024
NG = CH // 128
RANK = 512
LOWW = RANK + 128
NS = 16
ROWS = SEQS * TOK
HALF = TOK // 2
OWN = HALF // N_Y
EXROWS = (NS + 2) * 8


def mix_kernel(
    tail_hbm,
    cw_hbm,
    cb_hbm,
    xbc_hbm,
    dtb_hbm,
    decay_hbm,
    skip_hbm,
    x_hbm,
    xdt_hbm,
    init_hbm,
    dtw_hbm,
    z_hbm,
    w_hbm,
    res_hbm,
    out_ref,
    st_ref,
    tail_ref,
    cw_ref,
    cb_ref,
    xbc_ref,
    dtb_ref,
    decay_ref,
    skip_ref,
    x_ref,
    xdt_ref,
    init_ref,
    dtw_ref,
    z_ref,
    w_ref,
    res_ref,
    rim_out,
    rim_in,
    joined,
    act,
    xg,
    dtg,
    splat,
    pick,
    pre,
    rate_t,
    init_t,
    flip,
    lowp,
    lows,
    lowr,
    lown,
    exx,
    exz,
    before,
    since,
    ent,
    both,
    part,
    opp,
    fin,
    load_sem,
    rim_sem,
    lsib_sem,
    low_sem,
    nrm_sem,
    nsib_sem,
    exx_sem,
    exz_sem,
    wown_sem,
    wsib_sem,
    both_sem,
    opp_sem,
    fin_sem,
):
    q = lax.axis_index("seq")
    t = lax.axis_index("tp")
    z, x = q // N_X, lax.rem(q, N_X)
    y, core = t // 2, lax.rem(t, 2)

    sib = (q, y * 2 + 1 - core)

    def at_y(k):
        return (q, lax.rem(y + k, N_Y) * 2 + core)

    def at_x(k):
        return (z * N_X + lax.rem(x + k, N_X), t)

    def at_z(k):
        return (lax.rem(z + k, N_Z) * N_X + x, t)

    up, down = at_y(1), at_y(3)
    after = (lax.rem(q + 1, N_SEQ), t)
    prior = (lax.rem(q + N_SEQ - 1, N_SEQ), t)

    def remote(src, dst, sems, dev):
        return pltpu.make_async_remote_copy(
            src_ref=src, dst_ref=dst, send_sem=sems.at[0], recv_sem=sems.at[1], device_id=dev, device_id_type=MESH
        )

    barrier = pltpu.get_barrier_semaphore()
    peers = [prior, sib] + [at_y(k) for k in (1, 2, 3)]
    peers += [at_x(k) for k in (1, 2, 3)] + [at_z(k) for k in (1, 2, 3)]
    loads = [
        pltpu.make_async_copy(src, dst, load_sem.at[i])
        for i, (src, dst) in enumerate(
            (
                (x_hbm, x_ref),
                (cw_hbm, cw_ref),
                (cb_hbm, cb_ref),
                (tail_hbm, tail_ref),
                (xdt_hbm, xdt_ref),
                (xbc_hbm, xbc_ref),
                (decay_hbm, decay_ref),
                (dtb_hbm, dtb_ref),
                (skip_hbm, skip_ref),
                (dtw_hbm, dtw_ref),
                (init_hbm, init_ref),
                (z_hbm, z_ref),
                (res_hbm, res_ref),
            )
        )
    ]

    own_rows = pl.ds(pl.multiple_of(core * CH, CH), CH)

    def w_block(j):
        return pl.ds(pl.multiple_of(lax.rem(y + j, N_Y) * CH, CH), CH)

    def w_source(j, who):
        return w_hbm.at[:, pl.ds(pl.multiple_of((lax.rem(y + j, N_Y) * 2 + who) * CH, CH), CH)]

    def w_own(j):
        return pltpu.make_async_copy(w_source(j, core), w_ref.at[own_rows, w_block(j)], wown_sem.at[j])

    def w_give(j):
        return remote(w_source(j, 1 - core), w_ref.at[own_rows, w_block(j)], wsib_sem.at[j], sib)

    loads[0].start()
    for dev in peers:
        pl.semaphore_signal(barrier, inc=1, device_id=dev, device_id_type=MESH)
    for c in loads[1:]:
        c.start()
    for j in (2, 1, 3, 0):
        w_own(j).start()

    loads[0].wait()
    row8 = lax.broadcasted_iota(jnp.int32, (8, CH), 0)
    last = [x_ref[s, TOK - 16 : TOK, :].astype(F32)[8:16, :] for s in range(SEQS)]
    packed = [jnp.where(row8 < 4, pltpu.roll(last[s], 4, 0), last[s + 1]) for s in (0, 2)]
    rim_out[...] = jnp.concatenate(packed, axis=0).astype(BF16)

    pl.semaphore_wait(barrier, len(peers))
    rim = remote(rim_out, rim_in, rim_sem, after)
    rim.start()
    w_give(2).start()

    def conv_block(s, b):
        r = pl.multiple_of(b * 16, 16)
        window = joined[s, pl.ds(r, 24), :]
        mixed = cb_ref[...] + cw_ref[0:1, :] * window[5:21, :]
        for k in range(1, 4):
            mixed = mixed + cw_ref[k : k + 1, :] * window[5 + k : 21 + k, :]
        rounded = (mixed / (1.0 + jnp.exp(-mixed))).astype(BF16)
        act[pl.ds(pl.multiple_of(s * TOK + r, 16), 16), :] = rounded
        wide = rounded.astype(F32)
        for h in range(2):
            base = pl.multiple_of((s * (TOK // 8) + b * 2 + h) * 64, 64)
            for c in range(NG):
                xg[pl.ds(base + c * 8, 8), :] = wide[h * 8 : h * 8 + 8, c * 128 : (c + 1) * 128]

    loads[1].wait()
    loads[2].wait()

    @pl.loop(0, SEQS)
    def _(s):
        @pl.loop(0, TOK // 16)
        def _(b):
            r = pl.multiple_of(b * 16, 16)
            joined[s, pl.ds(r + 8, 16), :] = x_ref[s, pl.ds(r, 16), :].astype(F32)

        @pl.loop(1, TOK // 16)
        def _(b):
            conv_block(s, b)

    for s in range(SEQS):
        lowp[s, :, RANK:] = jnp.zeros((TOK, LOWW - RANK), BF16)

    half = pl.ds(pl.multiple_of(core * HALF, HALF), HALF)
    other = pl.ds(pl.multiple_of((1 - core) * HALF, HALF), HALF)
    mine = pl.ds(pl.multiple_of(core * HALF + y * OWN, OWN), OWN)

    def share(k):
        return pl.ds(pl.multiple_of(lax.rem(y + k, N_Y) * OWN, OWN), OWN)

    def lsib_copy(s):
        return remote(lowp.at[s, other], lows.at[s], lsib_sem.at[s], sib)

    def low_copy(s, k):
        return remote(lows.at[s, share(k)], lowr.at[s, k - 1], low_sem.at[s, k - 1], at_y(k))

    def nrm_copy(s, k):
        return remote(lown.at[s, mine], lown.at[s, mine], nrm_sem.at[s, k - 1], at_y(k))

    def nsib_copy(s):
        return remote(lown.at[s, half], lown.at[s, half], nsib_sem.at[s], sib)

    def exx_copy(s, k):
        return remote(exx.at[s, x], exx.at[s, x], exx_sem.at[s, k - 1], at_x(k))

    def exz_copy(s, k):
        return remote(exz.at[s, z], exz.at[s, z], exz_sem.at[s, k - 1], at_z(k))

    def low_partial(s):
        conv_block(s, 0)
        rows = act[s * TOK : (s + 1) * TOK, :]
        lowp[s, :, 0:RANK] = jnp.dot(rows, xdt_ref[...], preferred_element_type=F32).astype(BF16)
        lowp[s, :, RANK : RANK + 2 * NS] = lax.dot_general(
            rows, xbc_ref[...], (((1,), (1,)), ((), ())), preferred_element_type=F32
        ).astype(BF16)
        lsib_copy(s).start()

    def low_pair(s):
        lsib_copy(s).wait_recv()
        lows[s] = (lows[s].astype(F32) + lowp[s, half, :].astype(F32)).astype(BF16)
        for k in (2, 1, 3):
            low_copy(s, k).start()

    def normalise(s):
        total = lows[s, share(0), :].astype(F32)
        for k in range(1, N_Y):
            low_copy(s, k).wait_recv()
        for k in range(1, N_Y):
            total = total + lowr[s, k - 1].astype(F32)
        low = total[:, :RANK]
        scale = lax.rsqrt(jnp.mean(low * low, axis=-1, keepdims=True) + 1e-6)
        lown[s, mine, 0:RANK] = (low * scale).astype(BF16)
        bc = total[:, RANK:]
        high = bc.astype(BF16).astype(F32)
        lown[s, mine, RANK:] = (high + pltpu.roll(bc - high, 2 * NS, 1)).astype(BF16)
        for k in (2, 1, 3):
            nrm_copy(s, k).start()

    def low_forward(s):
        for k in range(1, N_Y):
            nrm_copy(s, k).wait_recv()
        nsib_copy(s).start()

    def steps(s):
        nsib_copy(s).wait_recv()
        if s == 0:
            loads[9].wait()
        pre[...] = jnp.dot(lown[s, :, 0:RANK], dtw_ref[...], preferred_element_type=F32)

        @pl.loop(0, TOK // 16)
        def _(b):
            r = pl.multiple_of(b * 16, 16)
            v = pre[pl.ds(r, 16), :] + dtb_ref[...]
            dt = jnp.maximum(v, 0.0) + jnp.log1p(jnp.exp(-jnp.abs(v)))
            for h in range(2):
                base = pl.multiple_of((s * (TOK // 8) + b * 2 + h) * 64, 64)
                for c in range(NG):
                    dtg[pl.ds(base + c * 8, 8), :] = dt[h * 8 : h * 8 + 8, c * 128 : (c + 1) * 128]

        maps = lown[s, :, RANK:]
        for p in range(2 * NS // 8):
            wide = jnp.dot(maps, pick[:, p * 1024 : (p + 1) * 1024], preferred_element_type=F32)
            for i in range(8):
                at = (p * 8 + i) * ROWS + s * TOK
                splat[at : at + TOK, :] = wide[:, i * 128 : (i + 1) * 128]

    def put_states(dst, s, i, states, elapsed):
        for m in range(NS // 2):
            dst[s, i, m * 16 : (m + 1) * 16, :] = jnp.concatenate(states[2 * m : 2 * m + 2], axis=0).astype(BF16)
        high = elapsed.astype(BF16).astype(F32)
        dst[s, i, NS * 8 :, :] = jnp.concatenate([high, elapsed - high], axis=0).astype(BF16)

    def get_elapsed(src, s, i):
        parts = src[s, i, NS * 8 :, :].astype(F32)
        return parts[0:8] + parts[8:16]

    def first_pass(s):
        rates = [rate_t[n] for n in range(NS)]

        def block(b, carry):
            h, elapsed = list(carry[0]), carry[1]
            base = pl.multiple_of((s * (TOK // 8) + b) * 64, 64)
            for i in range(8):
                dt = dtg[pl.ds(base + i, 8, stride=8), :]
                u = dt * xg[pl.ds(base + i, 8, stride=8), :]
                elapsed = elapsed + dt
                tok = s * TOK + b * 8 + i
                for n in range(NS):
                    h[n] = jnp.exp2(rates[n] * dt) * h[n] + splat[pl.ds(n * ROWS + tok, 1), :] * u
            return (tuple(h), elapsed)

        zero = jnp.zeros((8, 128), F32)
        h, elapsed = lax.fori_loop(0, TOK // 8, block, ((zero,) * NS, zero))
        put_states(exx, s, x, h, elapsed)
        for k in (2, 1, 3):
            exx_copy(s, k).start()

    def along_x(s):
        for k in range(1, N_X):
            exx_copy(s, k).wait_recv()
        spans = [get_elapsed(exx, s, i) for i in range(N_X)]
        totals = []
        for m in range(NS // 2):
            pairs = [exx[s, i, m * 16 : (m + 1) * 16, :].astype(F32) for i in range(N_X)]
            for h in range(2):
                n = 2 * m + h
                state = pairs[0][h * 8 : h * 8 + 8]
                kept = jnp.where(x == 1, state, jnp.zeros_like(state))
                for i in range(1, N_X):
                    state = jnp.exp2(rate_t[n] * spans[i]) * state + pairs[i][h * 8 : h * 8 + 8]
                    if i < N_X - 1:
                        kept = jnp.where(x == i + 1, state, kept)
                before[s, n] = kept
                totals.append(state)
        span = spans[0]
        kept = jnp.where(x == 1, span, jnp.zeros_like(span))
        for i in range(1, N_X):
            span = span + spans[i]
            if i < N_X - 1:
                kept = jnp.where(x == i + 1, span, kept)
        since[s] = kept
        put_states(exz, s, z, totals, span)
        for k in (2, 1, 3):
            exz_copy(s, k).start()

    def along_z(s):
        for k in range(1, N_Z):
            exz_copy(s, k).wait_recv()
        spans = [get_elapsed(exz, s, i) for i in range(N_Z - 1)]
        last_span = since[s]
        for m in range(NS // 2):
            pairs = [exz[s, i, m * 16 : (m + 1) * 16, :].astype(F32) for i in range(N_Z - 1)]
            for h in range(2):
                n = 2 * m + h
                rate = rate_t[n]
                state = init_t[s, n]
                for i in range(N_Z - 1):
                    later = jnp.exp2(rate * spans[i]) * state + pairs[i][h * 8 : h * 8 + 8]
                    state = jnp.where(i < z, later, state)
                ent[s, n] = jnp.exp2(rate * last_span) * state + before[s, n]

    def second_pass(s):
        rates = [rate_t[n] for n in range(NS)]
        skip = skip_ref[...]

        def block(b, h):
            h = list(h)
            base = pl.multiple_of((s * (TOK // 8) + b) * 64, 64)
            for i in range(8):
                dt = dtg[pl.ds(base + i, 8, stride=8), :]
                v = xg[pl.ds(base + i, 8, stride=8), :]
                u = dt * v
                tok = s * TOK + b * 8 + i
                total = skip * v
                for n in range(NS):
                    h[n] = jnp.exp2(rates[n] * dt) * h[n] + splat[pl.ds(n * ROWS + tok, 1), :] * u
                    total = total + splat[pl.ds((NS + n) * ROWS + tok, 1), :] * h[n]
                xg[pl.ds(base + i, 8, stride=8), :] = total
            return tuple(h)

        h = lax.fori_loop(0, TOK // 8, block, tuple(ent[s, n] for n in range(NS)))
        for nb in range(NS // 8):
            for i in range(8):
                flip[pl.ds(i, 8, stride=8), :] = h[nb * 8 + i]
            for c in range(NG):
                st_ref[0, s, nb * 8 : nb * 8 + 8, c * 128 : (c + 1) * 128] = flip[c * 8 : (c + 1) * 8, :]

    def gate(s):
        @pl.loop(0, TOK // 16)
        def _(b):
            r = pl.multiple_of(b * 16, 16)
            v = z_ref[s, pl.ds(r, 16), :].astype(F32)
            sz = v / (1.0 + jnp.exp(-v))
            base = pl.multiple_of((s * (TOK // 8) + b * 2) * 64, 64)
            for c in range(NG):
                scanned = jnp.concatenate(
                    [xg[pl.ds(base + c * 8, 8), :], xg[pl.ds(base + 64 + c * 8, 8), :]], axis=0
                )
                both[s, pl.ds(r, 16), pl.ds(pl.multiple_of(core * CH + c * 128, 128), 128)] = (
                    scanned * sz[:, c * 128 : (c + 1) * 128]
                ).astype(BF16)

    lo, hi = pl.ds(0, HALF), pl.ds(HALF, HALF)

    def both_copy(s):
        return remote(both.at[s, :, own_rows], both.at[s, :, own_rows], both_sem.at[s], sib)

    def opp_up(s):
        return remote(part.at[s, 2, lo], opp.at[s, 0], opp_sem.at[s, 0], up)

    def opp_down(s):
        return remote(part.at[s, 2, hi], opp.at[s, 1], opp_sem.at[s, 1], down)

    def own_up(s):
        return remote(part.at[s, 1, hi], fin.at[s, 0, hi], fin_sem.at[s, 0], up)

    def own_down(s):
        return remote(part.at[s, 3, lo], fin.at[s, 1, lo], fin_sem.at[s, 1], down)

    def fwd_up(s):
        return remote(part.at[s, 1, lo], fin.at[s, 0, lo], fin_sem.at[s, 2], up)

    def fwd_down(s):
        return remote(part.at[s, 3, hi], fin.at[s, 1, hi], fin_sem.at[s, 3], down)

    def for_chip(s, j):
        if s == 0:
            w_own(j).wait()
            w_give(j).wait_recv()
        part[s, j] = jnp.dot(both[s], w_ref[:, w_block(j)], preferred_element_type=F32).astype(BF16)
        if j == 2:
            opp_up(s).start()
            opp_down(s).start()
        if j == 1:
            own_up(s).start()
        if j == 3:
            own_down(s).start()

    def forward(s):
        for d in range(2):
            (opp_up(s) if d == 0 else opp_down(s)).wait_recv()
            j, r0 = (1, 0) if d == 0 else (3, HALF)

            @pl.loop(0, HALF // 16)
            def _(b):
                r = pl.multiple_of(b * 16, 16)
                here = part[s, j, pl.ds(r0 + r, 16), :].astype(F32)
                part[s, j, pl.ds(r0 + r, 16), :] = (here + opp[s, d, pl.ds(r, 16), :].astype(F32)).astype(BF16)

            (fwd_up(s) if d == 0 else fwd_down(s)).start()

    def finish(s):
        for c in (own_up(s), own_down(s), fwd_up(s), fwd_down(s)):
            c.wait_recv()

        @pl.loop(0, TOK // 16)
        def _(b):
            r = pl.ds(pl.multiple_of(b * 16, 16), 16)
            total = res_ref[s, r, :].astype(F32) + part[s, 0, r, :].astype(F32)
            total = total + fin[s, 0, r, :].astype(F32) + fin[s, 1, r, :].astype(F32)
            out_ref[s, r, :] = total.astype(BF16)

    def project(s):
        along_z(s)
        second_pass(s)
        if s == 0:
            loads[11].wait()
        gate(s)
        both_copy(s).start()

    def far(s):
        both_copy(s).wait_recv()
        for_chip(s, 2)

    def near(s):
        for j in (1, 3, 0):
            for_chip(s, j)

    loads[3].wait()
    rim.wait()
    for s in range(SEQS):
        rows = rim_in[...].astype(F32)[(s // 2) * 8 : (s // 2) * 8 + 8, :]
        joined[s, 0:8, :] = pltpu.roll(rows, 4, 0) if s % 2 == 0 else rows

    @pl.when(q == 0)
    def _():
        for s in range(SEQS):
            joined[s, 5:8, :] = tail_ref[:, s, :].astype(F32)

    loads[4].wait()
    loads[5].wait()
    for s in range(SEQS):
        low_partial(s)
        if s > 0:
            low_pair(s - 1)
    low_pair(SEQS - 1)
    w_give(1).start()
    for s in range(SEQS):
        normalise(s)

    for i in (6, 7, 8):
        loads[i].wait()

    for nb in range(NS // 8):
        for c in range(NG):
            flip[c * 8 : (c + 1) * 8, :] = -jnp.exp(decay_ref[nb * 8 : nb * 8 + 8, c * 128 : (c + 1) * 128]) * LOG2E
        for i in range(8):
            rate_t[nb * 8 + i] = flip[pl.ds(i, 8, stride=8), :]

    for n in range(2 * NS):
        r = lax.broadcasted_iota(jnp.int32, (128, 128), 0)
        pick[:, n * 128 : (n + 1) * 128] = jnp.where((r == n) | (r == n + 2 * NS), 1.0, 0.0).astype(BF16)

    low_forward(0)
    w_give(3).start()
    low_forward(1)
    steps(0)
    first_pass(0)
    w_give(0).start()

    loads[10].wait()

    @pl.loop(0, SEQS)
    def _(s):
        for nb in range(NS // 8):
            for c in range(NG):
                flip[c * 8 : (c + 1) * 8, :] = init_ref[s, nb * 8 : nb * 8 + 8, c * 128 : (c + 1) * 128]
            for i in range(8):
                init_t[s, nb * 8 + i] = flip[pl.ds(i, 8, stride=8), :]

    low_forward(2)
    steps(1)
    first_pass(1)
    low_forward(3)
    along_x(0)
    steps(2)
    first_pass(2)
    along_x(1)
    project(0)
    steps(3)
    far(0)
    near(0)
    along_x(2)
    project(1)
    first_pass(3)
    forward(0)
    far(1)
    near(1)
    project(2)
    along_x(3)
    far(2)
    forward(1)
    near(2)
    loads[12].wait()
    finish(0)
    project(3)
    far(3)
    forward(2)
    near(3)
    finish(1)
    forward(3)
    finish(2)
    finish(3)

    for j in range(N_Y):
        w_give(j).wait_send()
    for s in range(SEQS):
        lsib_copy(s).wait_send()
        nsib_copy(s).wait_send()
        for k in range(1, N_Y):
            low_copy(s, k).wait_send()
            nrm_copy(s, k).wait_send()
            exx_copy(s, k).wait_send()
            exz_copy(s, k).wait_send()
        both_copy(s).wait_send()
        for c in (opp_up(s), opp_down(s), own_up(s), own_down(s), fwd_up(s), fwd_down(s)):
            c.wait_send()


def body(
    inner_x,
    inner_z,
    conv_tail,
    conv_weight,
    conv_bias,
    xproj_dt,
    xproj_bc,
    dt_weight,
    dt_bias,
    decay_log,
    skip_gain,
    out_weight,
    residual,
    init_state,
):
    vmem = pl.BlockSpec(memory_space=pltpu.VMEM)
    anym = pl.BlockSpec(memory_space=pl.ANY)
    dma = pltpu.SemaphoreType.DMA
    scratch = [
        pltpu.VMEM((3, SEQS, CH), BF16),
        pltpu.VMEM((4, CH), F32),
        pltpu.VMEM((1, CH), F32),
        pltpu.VMEM((2 * NS, CH), BF16),
        pltpu.VMEM((1, CH), F32),
        pltpu.VMEM((NS, CH), F32),
        pltpu.VMEM((8, 128), F32),
        pltpu.VMEM((SEQS, TOK, CH), BF16),
        pltpu.VMEM((CH, RANK), BF16),
        pltpu.VMEM((SEQS, NS, CH), F32),
        pltpu.VMEM((RANK, CH), BF16),
        pltpu.VMEM((SEQS, TOK, CH), BF16),
        pltpu.VMEM((2 * CH, N_Y * CH), BF16),
        pltpu.VMEM((SEQS, TOK, CH), BF16),
        pltpu.VMEM((16, CH), BF16),
        pltpu.VMEM((16, CH), BF16),
        pltpu.VMEM((SEQS, TOK + 8, CH), F32),
        pltpu.VMEM((ROWS, CH), BF16),
        pltpu.VMEM((ROWS * 8, 128), F32),
        pltpu.VMEM((ROWS * 8, 128), F32),
        pltpu.VMEM((2 * NS * ROWS, 128), F32),
        pltpu.VMEM((128, 2 * NS * 128), BF16),
        pltpu.VMEM((TOK, CH), F32),
        pltpu.VMEM((NS, 8, 128), F32),
        pltpu.VMEM((SEQS, NS, 8, 128), F32),
        pltpu.VMEM((64, 128), F32),
        pltpu.VMEM((SEQS, TOK, LOWW), BF16),
        pltpu.VMEM((SEQS, HALF, LOWW), BF16),
        pltpu.VMEM((SEQS, N_Y - 1, OWN, LOWW), BF16),
        pltpu.VMEM((SEQS, TOK, LOWW), BF16),
        pltpu.VMEM((SEQS, N_X, EXROWS, 128), BF16),
        pltpu.VMEM((SEQS, N_Z, EXROWS, 128), BF16),
        pltpu.VMEM((SEQS, NS, 8, 128), F32),
        pltpu.VMEM((SEQS, 8, 128), F32),
        pltpu.VMEM((SEQS, NS, 8, 128), F32),
        pltpu.VMEM((SEQS, TOK, 2 * CH), BF16),
        pltpu.VMEM((SEQS, N_Y, TOK, CH), BF16),
        pltpu.VMEM((SEQS, 2, HALF, CH), BF16),
        pltpu.VMEM((SEQS, 2, TOK, CH), BF16),
        dma((13,)),
        dma((2,)),
        dma((SEQS, 2)),
        dma((SEQS, N_Y - 1, 2)),
        dma((SEQS, N_Y - 1, 2)),
        dma((SEQS, 2)),
        dma((SEQS, N_X - 1, 2)),
        dma((SEQS, N_Z - 1, 2)),
        dma((N_Y,)),
        dma((N_Y, 2)),
        dma((SEQS, 2)),
        dma((SEQS, 2, 2)),
        dma((SEQS, 4, 2)),
    ]
    out, st = pl.pallas_call(
        mix_kernel,
        out_shape=(
            pltpu.VMEM((SEQS, TOK, CH), BF16),
            pltpu.VMEM((1, SEQS, NS, CH), F32),
        ),
        in_specs=[anym] * 14,
        out_specs=(vmem, vmem),
        scratch_shapes=scratch,
        compiler_params=pltpu.CompilerParams(
            collective_id=0, has_side_effects=True, vmem_limit_bytes=62 * 1024 * 1024
        ),
    )(
        jnp.transpose(conv_tail, (1, 0, 2)),
        conv_weight,
        conv_bias.reshape(1, CH),
        xproj_bc.T,
        dt_bias.reshape(1, CH),
        decay_log,
        skip_gain.reshape(8, 128),
        inner_x,
        xproj_dt,
        init_state,
        dt_weight,
        inner_z,
        out_weight,
        residual,
    )
    return out, st


def solution(mesh):
    in_specs = (
        P(None, "seq", "tp"),
        P(None, "seq", "tp"),
        P(None, None, "tp"),
        P(None, "tp"),
        P("tp"),
        P("tp", None),
        P("tp", None),
        P(None, "tp"),
        P("tp"),
        P(None, "tp"),
        P("tp"),
        P("tp", None),
        P(None, "seq", "tp"),
        P(None, None, "tp"),
    )
    out_specs = (P(None, "seq", "tp"), P("seq", None, None, "tp"))
    return jax.shard_map(body, mesh=mesh, in_specs=in_specs, out_specs=out_specs, check_vma=False)
```

```python
import jax
import jax.numpy as jnp
from jax import lax
from jax.experimental import pallas as pl
from jax.experimental.pallas import tpu as pltpu
from jax.sharding import PartitionSpec as P

MESH = pl.DeviceIdType.MESH
F32 = jnp.float32
BF16 = jnp.bfloat16
LOG2E = 1.4426950408889634

N_SEQ = 16
N_TP = 8
N_X = 4
N_Y = 4
N_Z = 4
SEQS = 4
TOK = 128
CH = 1024
NG = CH // 128
RANK = 512
LOWW = RANK + 128
NS = 16
ROWS = SEQS * TOK
HALF = TOK // 2
OWN = HALF // N_Y
EXROWS = (NS + 2) * 8


def mix_kernel(
    tail_hbm,
    cw_hbm,
    cb_hbm,
    xbc_hbm,
    dtb_hbm,
    decay_hbm,
    skip_hbm,
    x_hbm,
    xdt_hbm,
    init_hbm,
    dtw_hbm,
    z_hbm,
    w_hbm,
    res_hbm,
    out_ref,
    st_ref,
    tail_ref,
    cw_ref,
    cb_ref,
    xbc_ref,
    dtb_ref,
    decay_ref,
    skip_ref,
    x_ref,
    xdt_ref,
    init_ref,
    dtw_ref,
    z_ref,
    w_ref,
    res_ref,
    rim_out,
    rim_in,
    joined,
    act,
    xg,
    dtg,
    splat,
    pick,
    pre,
    rate_t,
    init_t,
    flip,
    lowp,
    lows,
    lowr,
    lown,
    exx,
    exz,
    before,
    since,
    ent,
    both,
    part,
    opp,
    fin,
    load_sem,
    rim_sem,
    lsib_sem,
    low_sem,
    nrm_sem,
    nsib_sem,
    exx_sem,
    exz_sem,
    wown_sem,
    wsib_sem,
    both_sem,
    opp_sem,
    fin_sem,
):
    q = lax.axis_index("seq")
    t = lax.axis_index("tp")
    z, x = q // N_X, lax.rem(q, N_X)
    y, core = t // 2, lax.rem(t, 2)

    sib = (q, y * 2 + 1 - core)

    def at_y(k):
        return (q, lax.rem(y + k, N_Y) * 2 + core)

    def at_x(k):
        return (z * N_X + lax.rem(x + k, N_X), t)

    def at_z(k):
        return (lax.rem(z + k, N_Z) * N_X + x, t)

    up, down = at_y(1), at_y(3)
    after = (lax.rem(q + 1, N_SEQ), t)
    prior = (lax.rem(q + N_SEQ - 1, N_SEQ), t)

    def remote(src, dst, sems, dev):
        return pltpu.make_async_remote_copy(
            src_ref=src, dst_ref=dst, send_sem=sems.at[0], recv_sem=sems.at[1], device_id=dev, device_id_type=MESH
        )

    barrier = pltpu.get_barrier_semaphore()
    peers = [prior, sib] + [at_y(k) for k in (1, 2, 3)]
    peers += [at_x(k) for k in (1, 2, 3)] + [at_z(k) for k in (1, 2, 3)]
    loads = [
        pltpu.make_async_copy(src, dst, load_sem.at[i])
        for i, (src, dst) in enumerate(
            (
                (x_hbm, x_ref),
                (cw_hbm, cw_ref),
                (cb_hbm, cb_ref),
                (tail_hbm, tail_ref),
                (xdt_hbm, xdt_ref),
                (xbc_hbm, xbc_ref),
                (decay_hbm, decay_ref),
                (dtb_hbm, dtb_ref),
                (skip_hbm, skip_ref),
                (dtw_hbm, dtw_ref),
                (init_hbm, init_ref),
                (z_hbm, z_ref),
                (res_hbm, res_ref),
            )
        )
    ]

    own_rows = pl.ds(pl.multiple_of(core * CH, CH), CH)

    def w_block(j):
        return pl.ds(pl.multiple_of(lax.rem(y + j, N_Y) * CH, CH), CH)

    def w_source(j, who):
        return w_hbm.at[:, pl.ds(pl.multiple_of((lax.rem(y + j, N_Y) * 2 + who) * CH, CH), CH)]

    def w_own(j):
        return pltpu.make_async_copy(w_source(j, core), w_ref.at[own_rows, w_block(j)], wown_sem.at[j])

    def w_give(j):
        return remote(w_source(j, 1 - core), w_ref.at[own_rows, w_block(j)], wsib_sem.at[j], sib)

    loads[0].start()
    for dev in peers:
        pl.semaphore_signal(barrier, inc=1, device_id=dev, device_id_type=MESH)
    for c in loads[1:]:
        c.start()
    for j in (2, 1, 3, 0):
        w_own(j).start()

    loads[0].wait()
    row8 = lax.broadcasted_iota(jnp.int32, (8, CH), 0)
    last = [x_ref[s, TOK - 16 : TOK, :].astype(F32)[8:16, :] for s in range(SEQS)]
    packed = [jnp.where(row8 < 4, pltpu.roll(last[s], 4, 0), last[s + 1]) for s in (0, 2)]
    rim_out[...] = jnp.concatenate(packed, axis=0).astype(BF16)

    pl.semaphore_wait(barrier, len(peers))
    rim = remote(rim_out, rim_in, rim_sem, after)
    rim.start()
    w_give(2).start()

    def conv_block(s, b):
        r = pl.multiple_of(b * 16, 16)
        window = joined[s, pl.ds(r, 24), :]
        mixed = cb_ref[...] + cw_ref[0:1, :] * window[5:21, :]
        for k in range(1, 4):
            mixed = mixed + cw_ref[k : k + 1, :] * window[5 + k : 21 + k, :]
        rounded = (mixed / (1.0 + jnp.exp(-mixed))).astype(BF16)
        act[pl.ds(pl.multiple_of(s * TOK + r, 16), 16), :] = rounded
        wide = rounded.astype(F32)
        for h in range(2):
            base = pl.multiple_of((s * (TOK // 8) + b * 2 + h) * 64, 64)
            for c in range(NG):
                xg[pl.ds(base + c * 8, 8), :] = wide[h * 8 : h * 8 + 8, c * 128 : (c + 1) * 128]

    loads[1].wait()
    loads[2].wait()

    @pl.loop(0, SEQS)
    def _(s):
        @pl.loop(0, TOK // 16)
        def _(b):
            r = pl.multiple_of(b * 16, 16)
            joined[s, pl.ds(r + 8, 16), :] = x_ref[s, pl.ds(r, 16), :].astype(F32)

        @pl.loop(1, TOK // 16)
        def _(b):
            conv_block(s, b)

    for s in range(SEQS):
        lowp[s, :, RANK:] = jnp.zeros((TOK, LOWW - RANK), BF16)

    half = pl.ds(pl.multiple_of(core * HALF, HALF), HALF)
    other = pl.ds(pl.multiple_of((1 - core) * HALF, HALF), HALF)
    mine = pl.ds(pl.multiple_of(core * HALF + y * OWN, OWN), OWN)

    def share(k):
        return pl.ds(pl.multiple_of(lax.rem(y + k, N_Y) * OWN, OWN), OWN)

    def lsib_copy(s):
        return remote(lowp.at[s, other], lows.at[s], lsib_sem.at[s], sib)

    def low_copy(s, k):
        return remote(lows.at[s, share(k)], lowr.at[s, k - 1], low_sem.at[s, k - 1], at_y(k))

    def nrm_copy(s, k):
        return remote(lown.at[s, mine], lown.at[s, mine], nrm_sem.at[s, k - 1], at_y(k))

    def nsib_copy(s):
        return remote(lown.at[s, half], lown.at[s, half], nsib_sem.at[s], sib)

    def exx_copy(s, k):
        return remote(exx.at[s, x], exx.at[s, x], exx_sem.at[s, k - 1], at_x(k))

    def exz_copy(s, k):
        return remote(exz.at[s, z], exz.at[s, z], exz_sem.at[s, k - 1], at_z(k))

    def low_partial(s):
        conv_block(s, 0)
        rows = act[s * TOK : (s + 1) * TOK, :]
        lowp[s, :, 0:RANK] = jnp.dot(rows, xdt_ref[...], preferred_element_type=F32).astype(BF16)
        lowp[s, :, RANK : RANK + 2 * NS] = lax.dot_general(
            rows, xbc_ref[...], (((1,), (1,)), ((), ())), preferred_element_type=F32
        ).astype(BF16)
        lsib_copy(s).start()

    def low_pair(s):
        lsib_copy(s).wait_recv()
        lows[s] = (lows[s].astype(F32) + lowp[s, half, :].astype(F32)).astype(BF16)
        for k in (2, 1, 3):
            low_copy(s, k).start()

    def normalise(s):
        total = lows[s, share(0), :].astype(F32)
        for k in range(1, N_Y):
            low_copy(s, k).wait_recv()
        for k in range(1, N_Y):
            total = total + lowr[s, k - 1].astype(F32)
        low = total[:, :RANK]
        scale = lax.rsqrt(jnp.mean(low * low, axis=-1, keepdims=True) + 1e-6)
        lown[s, mine, 0:RANK] = (low * scale).astype(BF16)
        bc = total[:, RANK:]
        high = bc.astype(BF16).astype(F32)
        lown[s, mine, RANK:] = (high + pltpu.roll(bc - high, 2 * NS, 1)).astype(BF16)
        for k in (2, 1, 3):
            nrm_copy(s, k).start()

    def low_forward(s):
        for k in range(1, N_Y):
            nrm_copy(s, k).wait_recv()
        nsib_copy(s).start()

    def steps(s):
        nsib_copy(s).wait_recv()
        if s == 0:
            loads[9].wait()
        pre[...] = jnp.dot(lown[s, :, 0:RANK], dtw_ref[...], preferred_element_type=F32)

        @pl.loop(0, TOK // 16)
        def _(b):
            r = pl.multiple_of(b * 16, 16)
            v = pre[pl.ds(r, 16), :] + dtb_ref[...]
            dt = jnp.maximum(v, 0.0) + jnp.log1p(jnp.exp(-jnp.abs(v)))
            for h in range(2):
                base = pl.multiple_of((s * (TOK // 8) + b * 2 + h) * 64, 64)
                for c in range(NG):
                    dtg[pl.ds(base + c * 8, 8), :] = dt[h * 8 : h * 8 + 8, c * 128 : (c + 1) * 128]

        maps = lown[s, :, RANK:]
        for p in range(2 * NS // 8):
            wide = jnp.dot(maps, pick[:, p * 1024 : (p + 1) * 1024], preferred_element_type=F32)
            for i in range(8):
                at = (p * 8 + i) * ROWS + s * TOK
                splat[at : at + TOK, :] = wide[:, i * 128 : (i + 1) * 128]

    def put_states(dst, s, i, states, elapsed):
        for m in range(NS // 2):
            dst[s, i, m * 16 : (m + 1) * 16, :] = jnp.concatenate(states[2 * m : 2 * m + 2], axis=0).astype(BF16)
        high = elapsed.astype(BF16).astype(F32)
        dst[s, i, NS * 8 :, :] = jnp.concatenate([high, elapsed - high], axis=0).astype(BF16)

    def get_elapsed(src, s, i):
        parts = src[s, i, NS * 8 :, :].astype(F32)
        return parts[0:8] + parts[8:16]

    def first_pass(s):
        rates = [rate_t[n] for n in range(NS)]

        def block(b, carry):
            h, elapsed = list(carry[0]), carry[1]
            base = pl.multiple_of((s * (TOK // 8) + b) * 64, 64)
            for i in range(8):
                dt = dtg[pl.ds(base + i, 8, stride=8), :]
                u = dt * xg[pl.ds(base + i, 8, stride=8), :]
                elapsed = elapsed + dt
                tok = s * TOK + b * 8 + i
                for n in range(NS):
                    h[n] = jnp.exp2(rates[n] * dt) * h[n] + splat[pl.ds(n * ROWS + tok, 1), :] * u
            return (tuple(h), elapsed)

        zero = jnp.zeros((8, 128), F32)
        h, elapsed = lax.fori_loop(0, TOK // 8, block, ((zero,) * NS, zero))
        put_states(exx, s, x, h, elapsed)
        for k in (2, 1, 3):
            exx_copy(s, k).start()

    def along_x(s):
        for k in range(1, N_X):
            exx_copy(s, k).wait_recv()
        spans = [get_elapsed(exx, s, i) for i in range(N_X)]
        totals = []
        for m in range(NS // 2):
            pairs = [exx[s, i, m * 16 : (m + 1) * 16, :].astype(F32) for i in range(N_X)]
            for h in range(2):
                n = 2 * m + h
                state = pairs[0][h * 8 : h * 8 + 8]
                kept = jnp.where(x == 1, state, jnp.zeros_like(state))
                for i in range(1, N_X):
                    state = jnp.exp2(rate_t[n] * spans[i]) * state + pairs[i][h * 8 : h * 8 + 8]
                    if i < N_X - 1:
                        kept = jnp.where(x == i + 1, state, kept)
                before[s, n] = kept
                totals.append(state)
        span = spans[0]
        kept = jnp.where(x == 1, span, jnp.zeros_like(span))
        for i in range(1, N_X):
            span = span + spans[i]
            if i < N_X - 1:
                kept = jnp.where(x == i + 1, span, kept)
        since[s] = kept
        put_states(exz, s, z, totals, span)
        for k in (2, 1, 3):
            exz_copy(s, k).start()

    def along_z(s):
        for k in range(1, N_Z):
            exz_copy(s, k).wait_recv()
        spans = [get_elapsed(exz, s, i) for i in range(N_Z - 1)]
        last_span = since[s]
        for m in range(NS // 2):
            pairs = [exz[s, i, m * 16 : (m + 1) * 16, :].astype(F32) for i in range(N_Z - 1)]
            for h in range(2):
                n = 2 * m + h
                rate = rate_t[n]
                state = init_t[s, n]
                for i in range(N_Z - 1):
                    later = jnp.exp2(rate * spans[i]) * state + pairs[i][h * 8 : h * 8 + 8]
                    state = jnp.where(i < z, later, state)
                ent[s, n] = jnp.exp2(rate * last_span) * state + before[s, n]

    def second_pass(s):
        rates = [rate_t[n] for n in range(NS)]
        skip = skip_ref[...]

        def block(b, h):
            h = list(h)
            base = pl.multiple_of((s * (TOK // 8) + b) * 64, 64)
            for i in range(8):
                dt = dtg[pl.ds(base + i, 8, stride=8), :]
                v = xg[pl.ds(base + i, 8, stride=8), :]
                u = dt * v
                tok = s * TOK + b * 8 + i
                total = skip * v
                for n in range(NS):
                    h[n] = jnp.exp2(rates[n] * dt) * h[n] + splat[pl.ds(n * ROWS + tok, 1), :] * u
                    total = total + splat[pl.ds((NS + n) * ROWS + tok, 1), :] * h[n]
                xg[pl.ds(base + i, 8, stride=8), :] = total
            return tuple(h)

        h = lax.fori_loop(0, TOK // 8, block, tuple(ent[s, n] for n in range(NS)))
        for nb in range(NS // 8):
            for i in range(8):
                flip[pl.ds(i, 8, stride=8), :] = h[nb * 8 + i]
            for c in range(NG):
                st_ref[0, s, nb * 8 : nb * 8 + 8, c * 128 : (c + 1) * 128] = flip[c * 8 : (c + 1) * 8, :]

    def gate(s):
        @pl.loop(0, TOK // 16)
        def _(b):
            r = pl.multiple_of(b * 16, 16)
            sz = joined[s, pl.ds(r + 8, 16), :]
            base = pl.multiple_of((s * (TOK // 8) + b * 2) * 64, 64)
            for c in range(NG):
                scanned = jnp.concatenate(
                    [xg[pl.ds(base + c * 8, 8), :], xg[pl.ds(base + 64 + c * 8, 8), :]], axis=0
                )
                both[s, pl.ds(r, 16), pl.ds(pl.multiple_of(core * CH + c * 128, 128), 128)] = (
                    scanned * sz[:, c * 128 : (c + 1) * 128]
                ).astype(BF16)

    lo, hi = pl.ds(0, HALF), pl.ds(HALF, HALF)

    def both_copy(s):
        return remote(both.at[s, :, own_rows], both.at[s, :, own_rows], both_sem.at[s], sib)

    def opp_up(s):
        return remote(part.at[s, 2, lo], opp.at[s, 0], opp_sem.at[s, 0], up)

    def opp_down(s):
        return remote(part.at[s, 2, hi], opp.at[s, 1], opp_sem.at[s, 1], down)

    def own_up(s):
        return remote(part.at[s, 1, hi], fin.at[s, 0, hi], fin_sem.at[s, 0], up)

    def own_down(s):
        return remote(part.at[s, 3, lo], fin.at[s, 1, lo], fin_sem.at[s, 1], down)

    def fwd_up(s):
        return remote(part.at[s, 1, lo], fin.at[s, 0, lo], fin_sem.at[s, 2], up)

    def fwd_down(s):
        return remote(part.at[s, 3, hi], fin.at[s, 1, hi], fin_sem.at[s, 3], down)

    def for_chip(s, j):
        if s == 0:
            w_own(j).wait()
            w_give(j).wait_recv()
        part[s, j] = jnp.dot(both[s], w_ref[:, w_block(j)], preferred_element_type=F32).astype(BF16)
        if j == 2:
            opp_up(s).start()
            opp_down(s).start()
        if j == 1:
            own_up(s).start()
        if j == 3:
            own_down(s).start()

    def forward(s):
        for d in range(2):
            (opp_up(s) if d == 0 else opp_down(s)).wait_recv()
            j, r0 = (1, 0) if d == 0 else (3, HALF)

            @pl.loop(0, HALF // 16)
            def _(b):
                r = pl.multiple_of(b * 16, 16)
                here = part[s, j, pl.ds(r0 + r, 16), :].astype(F32)
                part[s, j, pl.ds(r0 + r, 16), :] = (here + opp[s, d, pl.ds(r, 16), :].astype(F32)).astype(BF16)

            (fwd_up(s) if d == 0 else fwd_down(s)).start()

    def finish(s):
        for c in (own_up(s), own_down(s), fwd_up(s), fwd_down(s)):
            c.wait_recv()

        @pl.loop(0, TOK // 16)
        def _(b):
            r = pl.ds(pl.multiple_of(b * 16, 16), 16)
            total = res_ref[s, r, :].astype(F32) + part[s, 0, r, :].astype(F32)
            total = total + fin[s, 0, r, :].astype(F32) + fin[s, 1, r, :].astype(F32)
            out_ref[s, r, :] = total.astype(BF16)

    def project(s):
        along_z(s)
        second_pass(s)
        gate(s)
        both_copy(s).start()

    def far(s):
        both_copy(s).wait_recv()
        for_chip(s, 2)

    def near(s):
        for j in (1, 3, 0):
            for_chip(s, j)

    loads[3].wait()
    rim.wait()
    for s in range(SEQS):
        rows = rim_in[...].astype(F32)[(s // 2) * 8 : (s // 2) * 8 + 8, :]
        joined[s, 0:8, :] = pltpu.roll(rows, 4, 0) if s % 2 == 0 else rows

    @pl.when(q == 0)
    def _():
        for s in range(SEQS):
            joined[s, 5:8, :] = tail_ref[:, s, :].astype(F32)

    loads[4].wait()
    loads[5].wait()
    for s in range(SEQS):
        low_partial(s)
        if s > 0:
            low_pair(s - 1)
    low_pair(SEQS - 1)
    w_give(1).start()
    for s in range(SEQS):
        normalise(s)

    for i in (6, 7, 8):
        loads[i].wait()

    for nb in range(NS // 8):
        for c in range(NG):
            flip[c * 8 : (c + 1) * 8, :] = -jnp.exp(decay_ref[nb * 8 : nb * 8 + 8, c * 128 : (c + 1) * 128]) * LOG2E
        for i in range(8):
            rate_t[nb * 8 + i] = flip[pl.ds(i, 8, stride=8), :]

    for n in range(2 * NS):
        r = lax.broadcasted_iota(jnp.int32, (128, 128), 0)
        pick[:, n * 128 : (n + 1) * 128] = jnp.where((r == n) | (r == n + 2 * NS), 1.0, 0.0).astype(BF16)

    loads[11].wait()

    @pl.loop(0, SEQS)
    def _(s):
        @pl.loop(0, TOK // 16)
        def _(b):
            r = pl.multiple_of(b * 16, 16)
            v = z_ref[s, pl.ds(r, 16), :].astype(F32)
            joined[s, pl.ds(r + 8, 16), :] = v / (1.0 + jnp.exp(-v))

    low_forward(0)
    w_give(3).start()
    low_forward(1)
    steps(0)
    first_pass(0)
    w_give(0).start()

    loads[10].wait()

    @pl.loop(0, SEQS)
    def _(s):
        for nb in range(NS // 8):
            for c in range(NG):
                flip[c * 8 : (c + 1) * 8, :] = init_ref[s, nb * 8 : nb * 8 + 8, c * 128 : (c + 1) * 128]
            for i in range(8):
                init_t[s, nb * 8 + i] = flip[pl.ds(i, 8, stride=8), :]

    low_forward(2)
    steps(1)
    first_pass(1)
    low_forward(3)
    steps(2)
    along_x(0)
    first_pass(2)
    along_x(1)
    steps(3)
    project(0)
    along_x(2)
    first_pass(3)
    far(0)
    near(0)
    project(1)
    along_x(3)
    project(2)
    forward(0)
    far(1)
    near(1)
    project(3)
    far(2)
    near(2)
    forward(1)
    far(3)
    near(3)
    loads[12].wait()
    finish(0)
    forward(2)
    finish(1)
    forward(3)
    finish(2)
    finish(3)

    for j in range(N_Y):
        w_give(j).wait_send()
    for s in range(SEQS):
        lsib_copy(s).wait_send()
        nsib_copy(s).wait_send()
        for k in range(1, N_Y):
            low_copy(s, k).wait_send()
            nrm_copy(s, k).wait_send()
            exx_copy(s, k).wait_send()
            exz_copy(s, k).wait_send()
        both_copy(s).wait_send()
        for c in (opp_up(s), opp_down(s), own_up(s), own_down(s), fwd_up(s), fwd_down(s)):
            c.wait_send()


def body(
    inner_x,
    inner_z,
    conv_tail,
    conv_weight,
    conv_bias,
    xproj_dt,
    xproj_bc,
    dt_weight,
    dt_bias,
    decay_log,
    skip_gain,
    out_weight,
    residual,
    init_state,
):
    vmem = pl.BlockSpec(memory_space=pltpu.VMEM)
    anym = pl.BlockSpec(memory_space=pl.ANY)
    dma = pltpu.SemaphoreType.DMA
    scratch = [
        pltpu.VMEM((3, SEQS, CH), BF16),
        pltpu.VMEM((4, CH), F32),
        pltpu.VMEM((1, CH), F32),
        pltpu.VMEM((2 * NS, CH), BF16),
        pltpu.VMEM((1, CH), F32),
        pltpu.VMEM((NS, CH), F32),
        pltpu.VMEM((8, 128), F32),
        pltpu.VMEM((SEQS, TOK, CH), BF16),
        pltpu.VMEM((CH, RANK), BF16),
        pltpu.VMEM((SEQS, NS, CH), F32),
        pltpu.VMEM((RANK, CH), BF16),
        pltpu.VMEM((SEQS, TOK, CH), BF16),
        pltpu.VMEM((2 * CH, N_Y * CH), BF16),
        pltpu.VMEM((SEQS, TOK, CH), BF16),
        pltpu.VMEM((16, CH), BF16),
        pltpu.VMEM((16, CH), BF16),
        pltpu.VMEM((SEQS, TOK + 8, CH), F32),
        pltpu.VMEM((ROWS, CH), BF16),
        pltpu.VMEM((ROWS * 8, 128), F32),
        pltpu.VMEM((ROWS * 8, 128), F32),
        pltpu.VMEM((2 * NS * ROWS, 128), F32),
        pltpu.VMEM((128, 2 * NS * 128), BF16),
        pltpu.VMEM((TOK, CH), F32),
        pltpu.VMEM((NS, 8, 128), F32),
        pltpu.VMEM((SEQS, NS, 8, 128), F32),
        pltpu.VMEM((64, 128), F32),
        pltpu.VMEM((SEQS, TOK, LOWW), BF16),
        pltpu.VMEM((SEQS, HALF, LOWW), BF16),
        pltpu.VMEM((SEQS, N_Y - 1, OWN, LOWW), BF16),
        pltpu.VMEM((SEQS, TOK, LOWW), BF16),
        pltpu.VMEM((SEQS, N_X, EXROWS, 128), BF16),
        pltpu.VMEM((SEQS, N_Z, EXROWS, 128), BF16),
        pltpu.VMEM((SEQS, NS, 8, 128), F32),
        pltpu.VMEM((SEQS, 8, 128), F32),
        pltpu.VMEM((SEQS, NS, 8, 128), F32),
        pltpu.VMEM((SEQS, TOK, 2 * CH), BF16),
        pltpu.VMEM((SEQS, N_Y, TOK, CH), BF16),
        pltpu.VMEM((SEQS, 2, HALF, CH), BF16),
        pltpu.VMEM((SEQS, 2, TOK, CH), BF16),
        dma((13,)),
        dma((2,)),
        dma((SEQS, 2)),
        dma((SEQS, N_Y - 1, 2)),
        dma((SEQS, N_Y - 1, 2)),
        dma((SEQS, 2)),
        dma((SEQS, N_X - 1, 2)),
        dma((SEQS, N_Z - 1, 2)),
        dma((N_Y,)),
        dma((N_Y, 2)),
        dma((SEQS, 2)),
        dma((SEQS, 2, 2)),
        dma((SEQS, 4, 2)),
    ]
    out, st = pl.pallas_call(
        mix_kernel,
        out_shape=(
            pltpu.VMEM((SEQS, TOK, CH), BF16),
            pltpu.VMEM((1, SEQS, NS, CH), F32),
        ),
        in_specs=[anym] * 14,
        out_specs=(vmem, vmem),
        scratch_shapes=scratch,
        compiler_params=pltpu.CompilerParams(
            collective_id=0, has_side_effects=True, vmem_limit_bytes=62 * 1024 * 1024
        ),
    )(
        jnp.transpose(conv_tail, (1, 0, 2)),
        conv_weight,
        conv_bias.reshape(1, CH),
        xproj_bc.T,
        dt_bias.reshape(1, CH),
        decay_log,
        skip_gain.reshape(8, 128),
        inner_x,
        xproj_dt,
        init_state,
        dt_weight,
        inner_z,
        out_weight,
        residual,
    )
    return out, st


def solution(mesh):
    in_specs = (
        P(None, "seq", "tp"),
        P(None, "seq", "tp"),
        P(None, None, "tp"),
        P(None, "tp"),
        P("tp"),
        P("tp", None),
        P("tp", None),
        P(None, "tp"),
        P("tp"),
        P(None, "tp"),
        P("tp"),
        P("tp", None),
        P(None, "seq", "tp"),
        P(None, None, "tp"),
    )
    out_specs = (P(None, "seq", "tp"), P("seq", None, None, "tp"))
    return jax.shard_map(body, mesh=mesh, in_specs=in_specs, out_specs=out_specs, check_vma=False)
```

```python
import jax
import jax.numpy as jnp
from jax import lax
from jax.experimental import pallas as pl
from jax.experimental.pallas import tpu as pltpu
from jax.sharding import PartitionSpec as P

MESH = pl.DeviceIdType.MESH
F32 = jnp.float32
BF16 = jnp.bfloat16
LOG2E = 1.4426950408889634

N_SEQ = 16
N_TP = 8
N_X = 4
N_Y = 4
N_Z = 4
SEQS = 4
TOK = 128
CH = 1024
NG = CH // 128
RANK = 512
LOWW = RANK + 128
NS = 16
ROWS = SEQS * TOK
HALF = TOK // 2
OWN = HALF // N_Y
EXROWS = (NS + 2) * 8
ENDS = (0, SEQS - 1)


def mix_kernel(
    tail_hbm,
    cw_hbm,
    cb_hbm,
    xbc_hbm,
    dtb_hbm,
    decay_hbm,
    skip_hbm,
    x_hbm,
    xdt_hbm,
    init_hbm,
    dtw_hbm,
    z_hbm,
    w_hbm,
    res_hbm,
    out_ref,
    st_ref,
    tail_ref,
    cw_ref,
    cb_ref,
    xbc_ref,
    dtb_ref,
    decay_ref,
    skip_ref,
    x_ref,
    xdt_ref,
    init_ref,
    dtw_ref,
    z_ref,
    w_ref,
    res_ref,
    rim_out,
    rim_in,
    joined,
    act,
    xg,
    dtg,
    splat,
    pick,
    pre,
    rate_t,
    init_t,
    flip,
    lowp,
    lows,
    lowr,
    lown,
    exx,
    exz,
    before,
    since,
    ent,
    both,
    part,
    opp,
    fin,
    load_sem,
    rim_sem,
    lsib_sem,
    low_sem,
    nrm_sem,
    nsib_sem,
    exx_sem,
    exz_sem,
    wown_sem,
    wsib_sem,
    both_sem,
    opp_sem,
    fin_sem,
):
    q = lax.axis_index("seq")
    t = lax.axis_index("tp")
    z, x = q // N_X, lax.rem(q, N_X)
    y, core = t // 2, lax.rem(t, 2)

    sib = (q, y * 2 + 1 - core)

    def at_y(k):
        return (q, lax.rem(y + k, N_Y) * 2 + core)

    def at_x(k):
        return (z * N_X + lax.rem(x + k, N_X), t)

    def at_z(k):
        return (lax.rem(z + k, N_Z) * N_X + x, t)

    up, down = at_y(1), at_y(3)
    after = (lax.rem(q + 1, N_SEQ), t)
    prior = (lax.rem(q + N_SEQ - 1, N_SEQ), t)

    def remote(src, dst, sems, dev):
        return pltpu.make_async_remote_copy(
            src_ref=src, dst_ref=dst, send_sem=sems.at[0], recv_sem=sems.at[1], device_id=dev, device_id_type=MESH
        )

    barrier = pltpu.get_barrier_semaphore()
    peers = [prior, sib] + [at_y(k) for k in (1, 2, 3)]
    peers += [at_x(k) for k in (1, 2, 3)] + [at_z(k) for k in (1, 2, 3)]
    loads = [
        pltpu.make_async_copy(src, dst, load_sem.at[i])
        for i, (src, dst) in enumerate(
            (
                (x_hbm, x_ref),
                (cw_hbm, cw_ref),
                (cb_hbm, cb_ref),
                (tail_hbm, tail_ref),
                (xdt_hbm, xdt_ref),
                (xbc_hbm, xbc_ref),
                (decay_hbm, decay_ref),
                (dtb_hbm, dtb_ref),
                (skip_hbm, skip_ref),
                (dtw_hbm, dtw_ref),
                (init_hbm, init_ref),
                (z_hbm, z_ref),
                (res_hbm, res_ref),
            )
        )
    ]

    own_rows = pl.ds(pl.multiple_of(core * CH, CH), CH)

    def w_block(j):
        return pl.ds(pl.multiple_of(lax.rem(y + j, N_Y) * CH, CH), CH)

    def w_source(j, who):
        return w_hbm.at[:, pl.ds(pl.multiple_of((lax.rem(y + j, N_Y) * 2 + who) * CH, CH), CH)]

    def w_own(j):
        return pltpu.make_async_copy(w_source(j, core), w_ref.at[own_rows, w_block(j)], wown_sem.at[j])

    def w_give(j):
        return remote(w_source(j, 1 - core), w_ref.at[own_rows, w_block(j)], wsib_sem.at[j], sib)

    loads[0].start()
    for dev in peers:
        pl.semaphore_signal(barrier, inc=1, device_id=dev, device_id_type=MESH)
    for c in loads[1:]:
        c.start()
    for j in (2, 1, 3, 0):
        w_own(j).start()

    loads[0].wait()
    row8 = lax.broadcasted_iota(jnp.int32, (8, CH), 0)
    last = [x_ref[s, TOK - 16 : TOK, :].astype(F32)[8:16, :] for s in range(SEQS)]
    packed = [jnp.where(row8 < 4, pltpu.roll(last[s], 4, 0), last[s + 1]) for s in (0, 2)]
    rim_out[...] = jnp.concatenate(packed, axis=0).astype(BF16)

    pl.semaphore_wait(barrier, len(peers))
    rim = remote(rim_out, rim_in, rim_sem, after)
    rim.start()
    w_give(2).start()

    def conv_block(s, b):
        r = pl.multiple_of(b * 16, 16)
        window = joined[s, pl.ds(r, 24), :]
        mixed = cb_ref[...] + cw_ref[0:1, :] * window[5:21, :]
        for k in range(1, 4):
            mixed = mixed + cw_ref[k : k + 1, :] * window[5 + k : 21 + k, :]
        rounded = (mixed / (1.0 + jnp.exp(-mixed))).astype(BF16)
        act[pl.ds(pl.multiple_of(s * TOK + r, 16), 16), :] = rounded
        wide = rounded.astype(F32)
        for h in range(2):
            base = pl.multiple_of((s * (TOK // 8) + b * 2 + h) * 64, 64)
            for c in range(NG):
                xg[pl.ds(base + c * 8, 8), :] = wide[h * 8 : h * 8 + 8, c * 128 : (c + 1) * 128]

    loads[1].wait()
    loads[2].wait()

    @pl.loop(0, SEQS)
    def _(s):
        @pl.loop(0, TOK // 16)
        def _(b):
            r = pl.multiple_of(b * 16, 16)
            joined[s, pl.ds(r + 8, 16), :] = x_ref[s, pl.ds(r, 16), :].astype(F32)

        @pl.loop(1, TOK // 16)
        def _(b):
            conv_block(s, b)

    for s in range(SEQS):
        lowp[s, :, RANK:] = jnp.zeros((TOK, LOWW - RANK), BF16)

    half = pl.ds(pl.multiple_of(core * HALF, HALF), HALF)
    other = pl.ds(pl.multiple_of((1 - core) * HALF, HALF), HALF)
    mine = pl.ds(pl.multiple_of(core * HALF + y * OWN, OWN), OWN)

    def share(k):
        return pl.ds(pl.multiple_of(lax.rem(y + k, N_Y) * OWN, OWN), OWN)

    def lsib_copy(s):
        return remote(lowp.at[s, other], lows.at[s], lsib_sem.at[s], sib)

    def low_copy(s, k):
        return remote(lows.at[s, share(k)], lowr.at[s, k - 1], low_sem.at[s, k - 1], at_y(k))

    def nrm_copy(s, k):
        return remote(lown.at[s, mine], lown.at[s, mine], nrm_sem.at[s, k - 1], at_y(k))

    def nsib_copy(s):
        return remote(lown.at[s, half], lown.at[s, half], nsib_sem.at[s], sib)

    def exx_copy(s, k):
        return remote(exx.at[s, x], exx.at[s, x], exx_sem.at[s, k - 1], at_x(k))

    def exz_copy(s, k):
        return remote(exz.at[s, z], exz.at[s, z], exz_sem.at[s, k - 1], at_z(k))

    def low_partial(s):
        conv_block(s, 0)
        rows = act[s * TOK : (s + 1) * TOK, :]
        lowp[s, :, 0:RANK] = jnp.dot(rows, xdt_ref[...], preferred_element_type=F32).astype(BF16)
        lowp[s, :, RANK : RANK + 2 * NS] = lax.dot_general(
            rows, xbc_ref[...], (((1,), (1,)), ((), ())), preferred_element_type=F32
        ).astype(BF16)
        lsib_copy(s).start()

    def low_pair(s):
        lsib_copy(s).wait_recv()
        lows[s] = (lows[s].astype(F32) + lowp[s, half, :].astype(F32)).astype(BF16)
        for k in (2, 1, 3):
            low_copy(s, k).start()

    def normalise(s):
        total = lows[s, share(0), :].astype(F32)
        for k in range(1, N_Y):
            low_copy(s, k).wait_recv()
        for k in range(1, N_Y):
            total = total + lowr[s, k - 1].astype(F32)
        low = total[:, :RANK]
        scale = lax.rsqrt(jnp.mean(low * low, axis=-1, keepdims=True) + 1e-6)
        lown[s, mine, 0:RANK] = (low * scale).astype(BF16)
        bc = total[:, RANK:]
        high = bc.astype(BF16).astype(F32)
        lown[s, mine, RANK:] = (high + pltpu.roll(bc - high, 2 * NS, 1)).astype(BF16)
        for k in (2, 1, 3):
            nrm_copy(s, k).start()

    def low_forward(s):
        for k in range(1, N_Y):
            nrm_copy(s, k).wait_recv()
        nsib_copy(s).start()

    def steps(s):
        nsib_copy(s).wait_recv()
        if s == 0:
            loads[9].wait()
        pre[...] = jnp.dot(lown[s, :, 0:RANK], dtw_ref[...], preferred_element_type=F32)

        @pl.loop(0, TOK // 16)
        def _(b):
            r = pl.multiple_of(b * 16, 16)
            v = pre[pl.ds(r, 16), :] + dtb_ref[...]
            dt = jnp.maximum(v, 0.0) + jnp.log1p(jnp.exp(-jnp.abs(v)))
            for h in range(2):
                base = pl.multiple_of((s * (TOK // 8) + b * 2 + h) * 64, 64)
                for c in range(NG):
                    dtg[pl.ds(base + c * 8, 8), :] = dt[h * 8 : h * 8 + 8, c * 128 : (c + 1) * 128]

        maps = lown[s, :, RANK:]
        for p in range(2 * NS // 8):
            wide = jnp.dot(maps, pick[:, p * 1024 : (p + 1) * 1024], preferred_element_type=F32)
            for i in range(8):
                at = (p * 8 + i) * ROWS + s * TOK
                splat[at : at + TOK, :] = wide[:, i * 128 : (i + 1) * 128]

    def put_states(dst, s, i, states, elapsed):
        for m in range(NS // 2):
            dst[s, i, m * 16 : (m + 1) * 16, :] = jnp.concatenate(states[2 * m : 2 * m + 2], axis=0).astype(BF16)
        high = elapsed.astype(BF16).astype(F32)
        dst[s, i, NS * 8 :, :] = jnp.concatenate([high, elapsed - high], axis=0).astype(BF16)

    def get_elapsed(src, s, i):
        parts = src[s, i, NS * 8 :, :].astype(F32)
        return parts[0:8] + parts[8:16]

    def first_pass(s):
        rates = [rate_t[n] for n in range(NS)]

        def block(b, carry):
            h, elapsed = list(carry[0]), carry[1]
            base = pl.multiple_of((s * (TOK // 8) + b) * 64, 64)
            for i in range(8):
                dt = dtg[pl.ds(base + i, 8, stride=8), :]
                u = dt * xg[pl.ds(base + i, 8, stride=8), :]
                elapsed = elapsed + dt
                tok = s * TOK + b * 8 + i
                for n in range(NS):
                    h[n] = jnp.exp2(rates[n] * dt) * h[n] + splat[pl.ds(n * ROWS + tok, 1), :] * u
            return (tuple(h), elapsed)

        zero = jnp.zeros((8, 128), F32)
        h, elapsed = lax.fori_loop(0, TOK // 8, block, ((zero,) * NS, zero))
        put_states(exx, s, x, h, elapsed)
        for k in (2, 1, 3):
            exx_copy(s, k).start()

    def along_x(s):
        for k in range(1, N_X):
            exx_copy(s, k).wait_recv()
        spans = [get_elapsed(exx, s, i) for i in range(N_X)]
        totals = []
        for m in range(NS // 2):
            pairs = [exx[s, i, m * 16 : (m + 1) * 16, :].astype(F32) for i in range(N_X)]
            for h in range(2):
                n = 2 * m + h
                state = pairs[0][h * 8 : h * 8 + 8]
                kept = jnp.where(x == 1, state, jnp.zeros_like(state))
                for i in range(1, N_X):
                    state = jnp.exp2(rate_t[n] * spans[i]) * state + pairs[i][h * 8 : h * 8 + 8]
                    if i < N_X - 1:
                        kept = jnp.where(x == i + 1, state, kept)
                before[s, n] = kept
                totals.append(state)
        span = spans[0]
        kept = jnp.where(x == 1, span, jnp.zeros_like(span))
        for i in range(1, N_X):
            span = span + spans[i]
            if i < N_X - 1:
                kept = jnp.where(x == i + 1, span, kept)
        since[s] = kept
        put_states(exz, s, z, totals, span)
        for k in (2, 1, 3):
            exz_copy(s, k).start()

    def along_z(s):
        for k in range(1, N_Z):
            exz_copy(s, k).wait_recv()
        spans = [get_elapsed(exz, s, i) for i in range(N_Z - 1)]
        last_span = since[s]
        for m in range(NS // 2):
            pairs = [exz[s, i, m * 16 : (m + 1) * 16, :].astype(F32) for i in range(N_Z - 1)]
            for h in range(2):
                n = 2 * m + h
                rate = rate_t[n]
                state = init_t[s, n]
                for i in range(N_Z - 1):
                    later = jnp.exp2(rate * spans[i]) * state + pairs[i][h * 8 : h * 8 + 8]
                    state = jnp.where(i < z, later, state)
                ent[s, n] = jnp.exp2(rate * last_span) * state + before[s, n]

    def second_pass(s):
        rates = [rate_t[n] for n in range(NS)]
        skip = skip_ref[...]

        def block(b, h):
            h = list(h)
            base = pl.multiple_of((s * (TOK // 8) + b) * 64, 64)
            for i in range(8):
                dt = dtg[pl.ds(base + i, 8, stride=8), :]
                v = xg[pl.ds(base + i, 8, stride=8), :]
                u = dt * v
                tok = s * TOK + b * 8 + i
                total = skip * v
                for n in range(NS):
                    h[n] = jnp.exp2(rates[n] * dt) * h[n] + splat[pl.ds(n * ROWS + tok, 1), :] * u
                    total = total + splat[pl.ds((NS + n) * ROWS + tok, 1), :] * h[n]
                xg[pl.ds(base + i, 8, stride=8), :] = total
            return tuple(h)

        h = lax.fori_loop(0, TOK // 8, block, tuple(ent[s, n] for n in range(NS)))
        for nb in range(NS // 8):
            for i in range(8):
                flip[pl.ds(i, 8, stride=8), :] = h[nb * 8 + i]
            for c in range(NG):
                st_ref[0, s, nb * 8 : nb * 8 + 8, c * 128 : (c + 1) * 128] = flip[c * 8 : (c + 1) * 8, :]

    def gate(s):
        @pl.loop(0, TOK // 16)
        def _(b):
            r = pl.multiple_of(b * 16, 16)
            v = z_ref[s, pl.ds(r, 16), :].astype(F32)
            sz = v / (1.0 + jnp.exp(-v))
            base = pl.multiple_of((s * (TOK // 8) + b * 2) * 64, 64)
            for c in range(NG):
                scanned = jnp.concatenate(
                    [xg[pl.ds(base + c * 8, 8), :], xg[pl.ds(base + 64 + c * 8, 8), :]], axis=0
                )
                both[s, pl.ds(r, 16), pl.ds(pl.multiple_of(core * CH + c * 128, 128), 128)] = (
                    scanned * sz[:, c * 128 : (c + 1) * 128]
                ).astype(BF16)

    lo, hi = pl.ds(0, HALF), pl.ds(HALF, HALF)

    def both_copy(s):
        return remote(both.at[s, :, own_rows], both.at[s, :, own_rows], both_sem.at[s], sib)

    def opp_up(s):
        return remote(part.at[s, 2, lo], opp.at[s, 0], opp_sem.at[s, 0], up)

    def opp_down(s):
        return remote(part.at[s, 2, hi], opp.at[s, 1], opp_sem.at[s, 1], down)

    def own_up(s):
        return remote(part.at[s, 1, hi], fin.at[s, 0, hi], fin_sem.at[s, 0], up)

    def own_down(s):
        return remote(part.at[s, 3, lo], fin.at[s, 1, lo], fin_sem.at[s, 1], down)

    def fwd_up(s):
        return remote(part.at[s, 1, lo], fin.at[s, 0, lo], fin_sem.at[s, 2], up)

    def fwd_down(s):
        return remote(part.at[s, 3, hi], fin.at[s, 1, hi], fin_sem.at[s, 3], down)

    def for_chip(s, j):
        if s == 0:
            w_own(j).wait()
            w_give(j).wait_recv()
        part[s, j] = jnp.dot(both[s], w_ref[:, w_block(j)], preferred_element_type=F32).astype(BF16)
        if j == 2:
            opp_up(s).start()
            opp_down(s).start()
        if j == 1 and s not in ENDS:
            own_up(s).start()
        if j == 3 and s not in ENDS:
            own_down(s).start()

    def forward(s):
        for d in range(2):
            (opp_up(s) if d == 0 else opp_down(s)).wait_recv()
            j, r0 = (1, 0) if d == 0 else (3, HALF)

            @pl.loop(0, HALF // 16)
            def _(b):
                r = pl.multiple_of(b * 16, 16)
                here = part[s, j, pl.ds(r0 + r, 16), :].astype(F32)
                part[s, j, pl.ds(r0 + r, 16), :] = (here + opp[s, d, pl.ds(r, 16), :].astype(F32)).astype(BF16)

            (fwd_up(s) if d == 0 else fwd_down(s)).start()

    def finish(s):
        for c in (own_up(s), own_down(s), fwd_up(s), fwd_down(s)):
            c.wait_recv()

        @pl.loop(0, TOK // 16)
        def _(b):
            r = pl.ds(pl.multiple_of(b * 16, 16), 16)
            total = res_ref[s, r, :].astype(F32) + part[s, 0, r, :].astype(F32)
            total = total + fin[s, 0, r, :].astype(F32) + fin[s, 1, r, :].astype(F32)
            out_ref[s, r, :] = total.astype(BF16)

    def project(s):
        along_z(s)
        second_pass(s)
        if s == 0:
            loads[11].wait()
        gate(s)
        both_copy(s).start()

    def combine(s):
        both_copy(s).wait_recv()
        for j in (2, 1, 3, 0):
            for_chip(s, j)
        if s in ENDS:
            opp_up(s).wait_send()
            opp_down(s).wait_send()
            own_up(s).start()
            own_down(s).start()

    loads[3].wait()
    rim.wait()
    for s in range(SEQS):
        rows = rim_in[...].astype(F32)[(s // 2) * 8 : (s // 2) * 8 + 8, :]
        joined[s, 0:8, :] = pltpu.roll(rows, 4, 0) if s % 2 == 0 else rows

    @pl.when(q == 0)
    def _():
        for s in range(SEQS):
            joined[s, 5:8, :] = tail_ref[:, s, :].astype(F32)

    loads[4].wait()
    loads[5].wait()
    for s in range(SEQS):
        low_partial(s)
        if s > 0:
            low_pair(s - 1)
    low_pair(SEQS - 1)
    w_give(1).start()
    for s in range(SEQS):
        normalise(s)

    for i in (6, 7, 8):
        loads[i].wait()

    for nb in range(NS // 8):
        for c in range(NG):
            flip[c * 8 : (c + 1) * 8, :] = -jnp.exp(decay_ref[nb * 8 : nb * 8 + 8, c * 128 : (c + 1) * 128]) * LOG2E
        for i in range(8):
            rate_t[nb * 8 + i] = flip[pl.ds(i, 8, stride=8), :]

    for n in range(2 * NS):
        r = lax.broadcasted_iota(jnp.int32, (128, 128), 0)
        pick[:, n * 128 : (n + 1) * 128] = jnp.where((r == n) | (r == n + 2 * NS), 1.0, 0.0).astype(BF16)

    low_forward(0)
    w_give(3).start()
    low_forward(1)
    steps(0)
    first_pass(0)
    w_give(0).start()

    loads[10].wait()

    @pl.loop(0, SEQS)
    def _(s):
        for nb in range(NS // 8):
            for c in range(NG):
                flip[c * 8 : (c + 1) * 8, :] = init_ref[s, nb * 8 : nb * 8 + 8, c * 128 : (c + 1) * 128]
            for i in range(8):
                init_t[s, nb * 8 + i] = flip[pl.ds(i, 8, stride=8), :]

    low_forward(2)
    steps(1)
    first_pass(1)
    low_forward(3)
    along_x(0)
    steps(2)
    first_pass(2)
    along_x(1)
    project(0)
    steps(3)
    combine(0)
    along_x(2)
    project(1)
    forward(0)
    combine(1)
    first_pass(3)
    project(2)
    forward(1)
    along_x(3)
    combine(2)
    project(3)
    forward(2)
    combine(3)
    loads[12].wait()
    finish(0)
    finish(1)
    forward(3)
    finish(2)
    finish(3)

    for j in range(N_Y):
        w_give(j).wait_send()
    for s in range(SEQS):
        lsib_copy(s).wait_send()
        nsib_copy(s).wait_send()
        for k in range(1, N_Y):
            low_copy(s, k).wait_send()
            nrm_copy(s, k).wait_send()
            exx_copy(s, k).wait_send()
            exz_copy(s, k).wait_send()
        both_copy(s).wait_send()
        if s not in ENDS:
            opp_up(s).wait_send()
            opp_down(s).wait_send()
        for c in (own_up(s), own_down(s), fwd_up(s), fwd_down(s)):
            c.wait_send()


def body(
    inner_x,
    inner_z,
    conv_tail,
    conv_weight,
    conv_bias,
    xproj_dt,
    xproj_bc,
    dt_weight,
    dt_bias,
    decay_log,
    skip_gain,
    out_weight,
    residual,
    init_state,
):
    vmem = pl.BlockSpec(memory_space=pltpu.VMEM)
    anym = pl.BlockSpec(memory_space=pl.ANY)
    dma = pltpu.SemaphoreType.DMA
    scratch = [
        pltpu.VMEM((3, SEQS, CH), BF16),
        pltpu.VMEM((4, CH), F32),
        pltpu.VMEM((1, CH), F32),
        pltpu.VMEM((2 * NS, CH), BF16),
        pltpu.VMEM((1, CH), F32),
        pltpu.VMEM((NS, CH), F32),
        pltpu.VMEM((8, 128), F32),
        pltpu.VMEM((SEQS, TOK, CH), BF16),
        pltpu.VMEM((CH, RANK), BF16),
        pltpu.VMEM((SEQS, NS, CH), F32),
        pltpu.VMEM((RANK, CH), BF16),
        pltpu.VMEM((SEQS, TOK, CH), BF16),
        pltpu.VMEM((2 * CH, N_Y * CH), BF16),
        pltpu.VMEM((SEQS, TOK, CH), BF16),
        pltpu.VMEM((16, CH), BF16),
        pltpu.VMEM((16, CH), BF16),
        pltpu.VMEM((SEQS, TOK + 8, CH), F32),
        pltpu.VMEM((ROWS, CH), BF16),
        pltpu.VMEM((ROWS * 8, 128), F32),
        pltpu.VMEM((ROWS * 8, 128), F32),
        pltpu.VMEM((2 * NS * ROWS, 128), F32),
        pltpu.VMEM((128, 2 * NS * 128), BF16),
        pltpu.VMEM((TOK, CH), F32),
        pltpu.VMEM((NS, 8, 128), F32),
        pltpu.VMEM((SEQS, NS, 8, 128), F32),
        pltpu.VMEM((64, 128), F32),
        pltpu.VMEM((SEQS, TOK, LOWW), BF16),
        pltpu.VMEM((SEQS, HALF, LOWW), BF16),
        pltpu.VMEM((SEQS, N_Y - 1, OWN, LOWW), BF16),
        pltpu.VMEM((SEQS, TOK, LOWW), BF16),
        pltpu.VMEM((SEQS, N_X, EXROWS, 128), BF16),
        pltpu.VMEM((SEQS, N_Z, EXROWS, 128), BF16),
        pltpu.VMEM((SEQS, NS, 8, 128), F32),
        pltpu.VMEM((SEQS, 8, 128), F32),
        pltpu.VMEM((SEQS, NS, 8, 128), F32),
        pltpu.VMEM((SEQS, TOK, 2 * CH), BF16),
        pltpu.VMEM((SEQS, N_Y, TOK, CH), BF16),
        pltpu.VMEM((SEQS, 2, HALF, CH), BF16),
        pltpu.VMEM((SEQS, 2, TOK, CH), BF16),
        dma((13,)),
        dma((2,)),
        dma((SEQS, 2)),
        dma((SEQS, N_Y - 1, 2)),
        dma((SEQS, N_Y - 1, 2)),
        dma((SEQS, 2)),
        dma((SEQS, N_X - 1, 2)),
        dma((SEQS, N_Z - 1, 2)),
        dma((N_Y,)),
        dma((N_Y, 2)),
        dma((SEQS, 2)),
        dma((SEQS, 2, 2)),
        dma((SEQS, 4, 2)),
    ]
    out, st = pl.pallas_call(
        mix_kernel,
        out_shape=(
            pltpu.VMEM((SEQS, TOK, CH), BF16),
            pltpu.VMEM((1, SEQS, NS, CH), F32),
        ),
        in_specs=[anym] * 14,
        out_specs=(vmem, vmem),
        scratch_shapes=scratch,
        compiler_params=pltpu.CompilerParams(
            collective_id=0, has_side_effects=True, vmem_limit_bytes=62 * 1024 * 1024
        ),
    )(
        jnp.transpose(conv_tail, (1, 0, 2)),
        conv_weight,
        conv_bias.reshape(1, CH),
        xproj_bc.T,
        dt_bias.reshape(1, CH),
        decay_log,
        skip_gain.reshape(8, 128),
        inner_x,
        xproj_dt,
        init_state,
        dt_weight,
        inner_z,
        out_weight,
        residual,
    )
    return out, st


def solution(mesh):
    in_specs = (
        P(None, "seq", "tp"),
        P(None, "seq", "tp"),
        P(None, None, "tp"),
        P(None, "tp"),
        P("tp"),
        P("tp", None),
        P("tp", None),
        P(None, "tp"),
        P("tp"),
        P(None, "tp"),
        P("tp"),
        P("tp", None),
        P(None, "seq", "tp"),
        P(None, None, "tp"),
    )
    out_specs = (P(None, "seq", "tp"), P("seq", None, None, "tp"))
    return jax.shard_map(body, mesh=mesh, in_specs=in_specs, out_specs=out_specs, check_vma=False)
```
